32 devices in a mesh: morton: 4 (over z), slab: 8 (over y, x, core).
Axes of the slice: x: 2, y: 2, z: 4, core: 2. Of those that a mesh axis runs over, the one named last changes fastest.
Arguments:
- velocity: float32 [128, 64, 256], P('slab', 'morton'), may hold values from -6 to 6
Outputs:
- approx: float32 [32, 16, 64], P('slab', 'morton')
- detail_two: float32 [7, 32, 16, 64], P(None, 'slab', 'morton')
- detail_one: float32 [7, 64, 32, 128], P(None, 'slab', 'morton')
The draws below stay inside these ranges and needn't reach their ends.
All inputs are finite; a program needn't handle non-finite values.
Results may differ from the reference program's by a relative error of at most 0.00002.
Values sent between devices are 32-bit elements; how exact they have to be, the bound alone decides.
A program may use at most 64 MiB of HBM per device.

```python
import jax
import jax.numpy as jnp
from jax import lax

NZ = 256
NX = 128
NY = 64


def block_levels(stream_key, dims, shards, low, top_value):
    gain, own = 1.0, jax.random.fold_in(stream_key, 6)
    for axis_at, parts in shards:
        heights = jnp.exp(jax.random.uniform(jax.random.fold_in(own, axis_at), (parts,), jnp.float32, low / len(shards), top_value / len(shards)))
        gain = gain * jnp.repeat(heights, dims[axis_at] // parts).reshape([-1 if axis == axis_at else 1 for axis in range(len(dims))])
    return gain


def bell_draw(key, extent, spread, limit, pieces=(), kind=jnp.bfloat16):
    gain = block_levels(key, extent, pieces, -0.22, 0.18) if pieces else 1.0
    drawn = jax.random.normal(key, extent, jnp.float32) * spread * gain
    return jnp.minimum(jnp.maximum(drawn, -limit), limit).astype(kind)


def setup_inputs(seed: int = 0) -> dict:
    key_of = jax.random.split(jax.random.key(seed), 2)
    return {
        "velocity": bell_draw(key_of[0], (NX, NY, NZ), 1.0, 6.0, ((0, 8), (1, 4)), jnp.float32),
    }


LIFT_ALPHA = -1.586134342059924
LIFT_BETA = -0.052980118572961
LIFT_GAMMA = 0.882911075530934
LIFT_DELTA = 0.443506852043971
LIFT_SCALE = 1.149604398860241


def cut_range(values, start, stop, dimension):
    return lax.slice_in_dim(values, start, stop, axis=dimension)


def lifting(extended, dimension):
    halfway = extended.shape[dimension] // 2
    new_shape = extended.shape[:dimension] + (halfway, 2) + extended.shape[dimension + 1:]
    paired = extended.reshape(new_shape)
    even_part = lax.index_in_dim(paired, 0, dimension + 1, keepdims=False)
    odd_part = lax.index_in_dim(paired, 1, dimension + 1, keepdims=False)
    first_detail = cut_range(odd_part, 0, halfway - 1, dimension) + LIFT_ALPHA * (
        cut_range(even_part, 0, halfway - 1, dimension) + cut_range(even_part, 1, halfway, dimension))
    first_smooth = cut_range(even_part, 1, halfway - 1, dimension) + LIFT_BETA * (
        cut_range(first_detail, 0, halfway - 2, dimension) + cut_range(first_detail, 1, halfway - 1, dimension))
    second_detail = cut_range(first_detail, 1, halfway - 2, dimension) + LIFT_GAMMA * (
        cut_range(first_smooth, 0, halfway - 3, dimension) + cut_range(first_smooth, 1, halfway - 2, dimension))
    second_smooth = cut_range(first_smooth, 1, halfway - 3, dimension) + LIFT_DELTA * (
        cut_range(second_detail, 0, halfway - 4, dimension) + cut_range(second_detail, 1, halfway - 3, dimension))
    lowpass = second_smooth * LIFT_SCALE
    highpass = cut_range(second_detail, 1, halfway - 3, dimension) / LIFT_SCALE
    return lowpass, highpass


def mirrored(values, dimension):
    widths = [(0, 0)] * values.ndim
    widths[dimension] = (4, 4)
    return jnp.pad(values, widths, mode="reflect")


def one_level(volume):
    subbands = [volume]
    for dimension in range(3):
        refined = []
        for subband in subbands:
            lowpass, highpass = lifting(mirrored(subband, dimension), dimension)
            refined = refined + [lowpass, highpass]
        subbands = refined
    return subbands


def reference(velocity):
    level_one = one_level(velocity)
    level_two = one_level(level_one[0])
    return level_two[0], jnp.stack(level_two[1:]), jnp.stack(level_one[1:])
```

```python
import functools

import jax
import jax.numpy as jnp
import numpy as np
from jax import lax
from jax.experimental import pallas as pl
from jax.experimental.pallas import tpu as pltpu
from jax.sharding import PartitionSpec as P

LIFT_ALPHA = -1.586134342059924
LIFT_BETA = -0.052980118572961
LIFT_GAMMA = 0.882911075530934
LIFT_DELTA = 0.443506852043971
LIFT_SCALE = 1.149604398860241

MESH = pl.DeviceIdType.MESH
FACES = ((1, 0), (-1, 0), (0, 1), (0, -1))
CORNERS = ((1, 1), (1, -1), (-1, 1), (-1, -1))
WAYS = FACES + CORNERS
HIGHEST = lax.Precision.HIGHEST


def lift_matrix(n):
    x = np.pad(np.eye(n), ((4, 4), (0, 0)), mode="reflect")
    e, o = x[0::2], x[1::2]
    d1 = o[:-1] + LIFT_ALPHA * (e[:-1] + e[1:])
    s1 = e[1:-1] + LIFT_BETA * (d1[:-1] + d1[1:])
    d2 = d1[1:-1] + LIFT_GAMMA * (s1[:-1] + s1[1:])
    s2 = s1[1:-1] + LIFT_DELTA * (d2[:-1] + d2[1:])
    return s2 * LIFT_SCALE, d2[1:] / LIFT_SCALE


def low_rank(coupling, rank):
    rest, us, vs = coupling.copy(), [], []
    for _ in range(rank):
        i, j = np.unravel_index(np.argmax(np.abs(rest)), rest.shape)
        u, v = rest[:, j] / rest[i, j], rest[i, :].copy()
        us.append(u)
        vs.append(v)
        rest = rest - u[:, None] * v[None, :]
    assert np.abs(rest).max() < 1e-12
    return np.stack(us, 1), np.stack(vs, 0)


def block_maps(b):
    blocks = 5
    low, high = lift_matrix(blocks * b)
    low2, high2 = lift_matrix(blocks * b // 2)
    pairs = ((low, high, 2), (low2 @ low, high2 @ low, 4))
    levels = []
    for lows, highs, rank in pairs:
        n = lows.shape[0] // blocks

        def part(row, col):
            cols = slice(col * b, (col + 1) * b)
            rows = slice(row * n, (row + 1) * n)
            return np.concatenate([lows[rows, cols], highs[rows, cols]])

        for row in range(blocks):
            for col in range(blocks):
                if abs(row - col) > 1:
                    assert np.abs(part(row, col)).max() == 0
                elif row != col:
                    like = part(2, 2 + col - row)
                    assert np.abs(part(row, col) - like).max() < 1e-12
        assert np.abs(part(1, 1) - part(2, 2)).max() < 1e-12
        assert np.abs(part(3, 3) - part(2, 2)).max() < 1e-12
        own = [part(0, 0), part(2, 2), part(4, 4)]
        u_up, v_up = low_rank(part(2, 1), rank)
        u_down, v_down = low_rank(part(2, 3), rank)
        levels.append((own, {1: u_up, -1: u_down}, {1: v_up, -1: v_down}))
    return levels


@functools.lru_cache(maxsize=None)
def matrices(bx, by, nz):
    low, high = lift_matrix(nz)
    low2, high2 = lift_matrix(nz // 2)
    depth = np.concatenate([low, high, low2 @ low, high2 @ low]).T
    sends, spreads = [], []
    for level, pad in ((0, 1), (1, 2)):
        own_x, ux, vx = block_maps(bx)[level]
        own_y, uy, vy = block_maps(by)[level]
        nx, ny = own_x[0].shape[0], own_y[0].shape[0]
        eye_x, eye_y = np.eye(nx), np.eye(ny)
        spread = [np.kron(ux[dx] if dx else eye_x, uy[dy] if dy else eye_y) for dx, dy in WAYS]

        def by_band(m):
            m = m.reshape(2, nx // 2, 2, ny // 2, -1).transpose(0, 2, 1, 3, 4)
            m = np.pad(m, ((0, 0),) * 3 + ((0, (pad - 1) * (ny // 2)), (0, 0)))
            return m.reshape(-1, m.shape[-1])

        spreads.append(by_band(np.concatenate(spread, 1)).astype(np.float32))
        rows = []
        for cx in range(3):
            for cy in range(3):
                out = [
                    np.kron(vx[dx] if dx else own_x[cx], vy[dy] if dy else own_y[cy])
                    for dx, dy in WAYS
                ]
                out.append(by_band(np.kron(own_x[cx], own_y[cy])))
                rows.append(np.concatenate(out))
        sends.append(np.stack(rows).astype(np.float32))
    return depth.astype(np.float32), sends[0], sends[1], spreads[0], spreads[1]


FACE, CORNER = 96, 24
SLOTS = tuple((k * FACE, FACE) for k in range(4)) + tuple(
    (4 * FACE + k * CORNER, CORNER) for k in range(4)
)


def dot(a, b):
    return jnp.dot(a, b, precision=HIGHEST, preferred_element_type=jnp.float32)


def kernel(
    nx, ny, x_hbm, t_hbm, s1_hbm, s2_hbm, u1_hbm, u2_hbm, approx, two, one,
    x_v, t_v, s1_v, s2_v, u1_v, u2_v, out_buf, in_buf, load_sem, send_sem, recv_sem,
):
    px, py = lax.axis_index("slab"), lax.axis_index("morton")
    not_first_x, last_x = lax.div(px + (nx - 2), nx - 1), lax.div(px, nx - 1)
    not_first_y, last_y = lax.div(py + (ny - 2), ny - 1), lax.div(py, ny - 1)
    here = (not_first_x + last_x) * 3 + not_first_y + last_y
    has_x = {1: 1 - last_x, -1: not_first_x, 0: 1}
    has_y = {1: 1 - last_y, -1: not_first_y, 0: 1}

    def exists(dx, dy):
        return has_x[dx] * has_y[dy] == 1

    loads = [
        pltpu.make_async_copy(source, target, load_sem.at[k])
        for k, (source, target) in enumerate((
            (x_hbm, x_v), (t_hbm, t_v), (s1_hbm.at[here], s1_v),
            (s2_hbm.at[here], s2_v), (u1_hbm, u1_v), (u2_hbm, u2_v),
        ))
    ]
    for load in loads:
        load.start()

    barrier = pltpu.get_barrier_semaphore()
    for dx, dy in WAYS:
        @pl.when(exists(dx, dy))
        def _():
            pl.semaphore_signal(
                barrier, inc=1, device_id=(py + dy, px + dx), device_id_type=MESH
            )

    for (dx, dy), (start, size) in zip(WAYS, SLOTS):
        @pl.when(jnp.logical_not(exists(-dx, -dy)))
        def _():
            in_buf[start:start + size, :] = jnp.zeros((size, 128), jnp.float32)

    loads[0].wait()
    loads[1].wait()
    z = dot(x_v[...].reshape(256, 256), t_v[...])
    z1, z2 = z[:, :256], z[:, 256:]
    loads[2].wait()
    p1 = dot(s1_v[:144, :], z1)
    loads[3].wait()
    p2 = dot(s2_v[:192, :], z2)
    for k in range(4):
        at = k * FACE
        out_buf[at:at + 32, :] = p1[k * 32:k * 32 + 32, :128]
        out_buf[at + 32:at + 64, :] = p1[k * 32:k * 32 + 32, 128:]
        out_buf[at + 64:at + 96, :] = p2[k * 32:k * 32 + 32, :]
        at = 4 * FACE + k * CORNER
        out_buf[at:at + 4, :] = p1[128 + k * 4:132 + k * 4, :128]
        out_buf[at + 4:at + 8, :] = p1[128 + k * 4:132 + k * 4, 128:]
        out_buf[at + 8:at + 24, :] = p2[128 + k * 16:144 + k * 16, :]

    pl.semaphore_wait(
        barrier,
        (1 + has_x[1] + has_x[-1]) * (1 + has_y[1] + has_y[-1]) - 1,
    )

    def message(k):
        (dx, dy), (start, size) = WAYS[k], SLOTS[k]
        return pltpu.make_async_remote_copy(
            src_ref=out_buf.at[pl.ds(start, size)],
            dst_ref=in_buf.at[pl.ds(start, size)],
            send_sem=send_sem.at[k],
            recv_sem=recv_sem.at[k],
            device_id=(py + dy, px + dx),
            device_id_type=MESH,
        )

    order = (2, 3, 4, 5, 6, 7, 0, 1)
    for k in order:
        @pl.when(exists(*WAYS[k]))
        def _():
            message(k).start()

    own1 = dot(s1_v[144:, :], z1)
    own2 = dot(s2_v[192:, :], z2)
    loads[4].wait()
    loads[5].wait()

    for k in order:
        dx, dy = WAYS[k]

        @pl.when(exists(-dx, -dy))
        def _():
            message(k).wait_recv()

    halo1 = [
        jnp.concatenate(
            [in_buf[k * FACE:k * FACE + 32, :], in_buf[k * FACE + 32:k * FACE + 64, :]], axis=1
        )
        for k in range(4)
    ]
    halo2 = [in_buf[k * FACE + 64:k * FACE + 96, :] for k in range(4)]
    for k in range(4):
        at = 4 * FACE + k * CORNER
        halo1.append(jnp.concatenate([in_buf[at:at + 4, :], in_buf[at + 4:at + 8, :]], axis=1))
        halo2.append(in_buf[at + 8:at + 24, :])
    o2 = own2 + dot(u2_v[...], jnp.concatenate(halo2, axis=0))
    o1 = own1 + dot(u1_v[...], jnp.concatenate(halo1, axis=0))

    o2 = o2.reshape(4, 4, 8, 128)
    for band in range(4):
        for bz in range(2):
            part = o2[band, :, :4, bz * 64:bz * 64 + 64]
            if band + bz:
                two[2 * band + bz - 1] = part
                one[2 * band + bz - 1] = o1[
                    band * 64:band * 64 + 64, bz * 128:bz * 128 + 128
                ].reshape(8, 8, 128)
            else:
                approx[...] = part

    for k in order:
        @pl.when(exists(*WAYS[k]))
        def _():
            message(k).wait_send()


def per_device(nx, ny, velocity):
    bx, by, nz = velocity.shape
    consts = matrices(bx, by, nz)
    f32 = jnp.float32
    vmem = pl.BlockSpec(memory_space=pltpu.VMEM)
    tables = [pltpu.VMEM(c.shape[-2:], f32) for c in consts]
    return pl.pallas_call(
        functools.partial(kernel, nx, ny),
        out_shape=(
            jax.ShapeDtypeStruct((bx // 4, by // 4, nz // 4), f32),
            jax.ShapeDtypeStruct((7, bx // 4, by // 4, nz // 4), f32),
            jax.ShapeDtypeStruct((7, bx // 2, by // 2, nz // 2), f32),
        ),
        in_specs=[pl.BlockSpec(memory_space=pl.ANY)] * 6,
        out_specs=(vmem, vmem, vmem),
        scratch_shapes=[pltpu.VMEM((bx, by, nz), f32)]
        + tables
        + [
            pltpu.VMEM((4 * (FACE + CORNER), 128), f32),
            pltpu.VMEM((4 * (FACE + CORNER), 128), f32),
            pltpu.SemaphoreType.DMA((6,)),
            pltpu.SemaphoreType.DMA((8,)),
            pltpu.SemaphoreType.DMA((8,)),
        ],
        compiler_params=pltpu.CompilerParams(
            collective_id=0, has_side_effects=True, vmem_limit_bytes=60 * 1024 * 1024
        ),
    )(velocity, *[jnp.asarray(c) for c in consts])


def solution(mesh):
    placed = (P("slab", "morton", None),)
    return jax.shard_map(
        functools.partial(per_device, mesh.shape["slab"], mesh.shape["morton"]),
        mesh=mesh,
        in_specs=placed,
        out_specs=(
            P("slab", "morton", None),
            P(None, "slab", "morton", None),
            P(None, "slab", "morton", None),
        ),
        check_vma=False,
    )
```

```python
import functools

import jax
import jax.numpy as jnp
import numpy as np
from jax import lax
from jax.experimental import pallas as pl
from jax.experimental.pallas import tpu as pltpu
from jax.sharding import PartitionSpec as P

LIFT_ALPHA = -1.586134342059924
LIFT_BETA = -0.052980118572961
LIFT_GAMMA = 0.882911075530934
LIFT_DELTA = 0.443506852043971
LIFT_SCALE = 1.149604398860241

MESH = pl.DeviceIdType.MESH
FACES = ((1, 0), (-1, 0), (0, 1), (0, -1))
CORNERS = ((1, 1), (1, -1), (-1, 1), (-1, -1))
WAYS = FACES + CORNERS
HIGHEST = lax.Precision.HIGHEST


def lift_matrix(n):
    x = np.pad(np.eye(n), ((4, 4), (0, 0)), mode="reflect")
    e, o = x[0::2], x[1::2]
    d1 = o[:-1] + LIFT_ALPHA * (e[:-1] + e[1:])
    s1 = e[1:-1] + LIFT_BETA * (d1[:-1] + d1[1:])
    d2 = d1[1:-1] + LIFT_GAMMA * (s1[:-1] + s1[1:])
    s2 = s1[1:-1] + LIFT_DELTA * (d2[:-1] + d2[1:])
    return s2 * LIFT_SCALE, d2[1:] / LIFT_SCALE


def low_rank(coupling, rank):
    rest, us, vs = coupling.copy(), [], []
    for _ in range(rank):
        i, j = np.unravel_index(np.argmax(np.abs(rest)), rest.shape)
        u, v = rest[:, j] / rest[i, j], rest[i, :].copy()
        us.append(u)
        vs.append(v)
        rest = rest - u[:, None] * v[None, :]
    assert np.abs(rest).max() < 1e-12
    return np.stack(us, 1), np.stack(vs, 0)


def block_maps(b):
    blocks = 5
    low, high = lift_matrix(blocks * b)
    low2, high2 = lift_matrix(blocks * b // 2)
    pairs = ((low, high, 2), (low2 @ low, high2 @ low, 4))
    levels = []
    for lows, highs, rank in pairs:
        n = lows.shape[0] // blocks

        def part(row, col):
            cols = slice(col * b, (col + 1) * b)
            rows = slice(row * n, (row + 1) * n)
            return np.concatenate([lows[rows, cols], highs[rows, cols]])

        for row in range(blocks):
            for col in range(blocks):
                if abs(row - col) > 1:
                    assert np.abs(part(row, col)).max() == 0
                elif row != col:
                    like = part(2, 2 + col - row)
                    assert np.abs(part(row, col) - like).max() < 1e-12
        assert np.abs(part(1, 1) - part(2, 2)).max() < 1e-12
        assert np.abs(part(3, 3) - part(2, 2)).max() < 1e-12
        own = [part(0, 0), part(2, 2), part(4, 4)]
        u_up, v_up = low_rank(part(2, 1), rank)
        u_down, v_down = low_rank(part(2, 3), rank)
        levels.append((own, {1: u_up, -1: u_down}, {1: v_up, -1: v_down}))
    return levels


@functools.lru_cache(maxsize=None)
def matrices(bx, by, nz):
    low, high = lift_matrix(nz)
    low2, high2 = lift_matrix(nz // 2)
    depth = np.concatenate([low, high, low2 @ low, high2 @ low]).T
    sends, spreads = [], []
    for level, pad in ((0, 1), (1, 2)):
        own_x, ux, vx = block_maps(bx)[level]
        own_y, uy, vy = block_maps(by)[level]
        nx, ny = own_x[0].shape[0], own_y[0].shape[0]
        eye_x, eye_y = np.eye(nx), np.eye(ny)
        spread = [np.kron(ux[dx] if dx else eye_x, uy[dy] if dy else eye_y) for dx, dy in WAYS]

        def by_band(m):
            m = m.reshape(2, nx // 2, 2, ny // 2, -1).transpose(0, 2, 1, 3, 4)
            m = np.pad(m, ((0, 0),) * 3 + ((0, (pad - 1) * (ny // 2)), (0, 0)))
            return m.reshape(-1, m.shape[-1])

        spreads.append(by_band(np.concatenate(spread, 1)).astype(np.float32))
        rows = []
        for cx in range(3):
            for cy in range(3):
                out = [
                    np.kron(vx[dx] if dx else own_x[cx], vy[dy] if dy else own_y[cy])
                    for dx, dy in WAYS
                ]
                out.append(by_band(np.kron(own_x[cx], own_y[cy])))
                rows.append(np.concatenate(out))
        sends.append(np.stack(rows).astype(np.float32))
    return depth.astype(np.float32), sends[0], sends[1], spreads[0], spreads[1]


FACE, CORNER = 96, 24
SLOTS = tuple((k * FACE, FACE) for k in range(4)) + tuple(
    (4 * FACE + k * CORNER, CORNER) for k in range(4)
)


def dot(a, b):
    return jnp.dot(a, b, precision=HIGHEST, preferred_element_type=jnp.float32)


def kernel(
    nx, ny, x_hbm, t_hbm, s1_hbm, s2_hbm, u1_hbm, u2_hbm, approx, two, one,
    x_v, t_v, s1_v, s2_v, u1_v, u2_v, out_buf, in_buf, load_sem, send_sem, recv_sem,
):
    px, py = lax.axis_index("slab"), lax.axis_index("morton")
    not_first_x, last_x = lax.div(px + (nx - 2), nx - 1), lax.div(px, nx - 1)
    not_first_y, last_y = lax.div(py + (ny - 2), ny - 1), lax.div(py, ny - 1)
    here = (not_first_x + last_x) * 3 + not_first_y + last_y
    has_x = {1: 1 - last_x, -1: not_first_x, 0: 1}
    has_y = {1: 1 - last_y, -1: not_first_y, 0: 1}

    def exists(dx, dy):
        return has_x[dx] * has_y[dy] == 1

    loads = [
        pltpu.make_async_copy(source, target, load_sem.at[k])
        for k, (source, target) in enumerate((
            (x_hbm, x_v), (t_hbm, t_v), (s1_hbm.at[here], s1_v),
            (s2_hbm.at[here], s2_v), (u1_hbm, u1_v), (u2_hbm, u2_v),
        ))
    ]
    for load in loads:
        load.start()

    barrier = pltpu.get_barrier_semaphore()
    for dx, dy in WAYS:
        @pl.when(exists(dx, dy))
        def _():
            pl.semaphore_signal(
                barrier, inc=1, device_id=(py + dy, px + dx), device_id_type=MESH
            )

    for (dx, dy), (start, size) in zip(WAYS, SLOTS):
        @pl.when(jnp.logical_not(exists(-dx, -dy)))
        def _():
            in_buf[start:start + size, :] = jnp.zeros((size, 128), jnp.float32)

    loads[0].wait()
    loads[1].wait()
    z = dot(x_v[...].reshape(256, 256), t_v[...])
    z1, z2 = z[:, :256], z[:, 256:]
    loads[2].wait()
    p1 = dot(s1_v[:144, :], z1)
    loads[3].wait()
    p2 = dot(s2_v[:192, :], z2)
    for k in range(4):
        at = k * FACE
        out_buf[at:at + 32, :] = p1[k * 32:k * 32 + 32, :128]
        out_buf[at + 32:at + 64, :] = p1[k * 32:k * 32 + 32, 128:]
        out_buf[at + 64:at + 96, :] = p2[k * 32:k * 32 + 32, :]
        at = 4 * FACE + k * CORNER
        out_buf[at:at + 4, :] = p1[128 + k * 4:132 + k * 4, :128]
        out_buf[at + 4:at + 8, :] = p1[128 + k * 4:132 + k * 4, 128:]
        out_buf[at + 8:at + 24, :] = p2[128 + k * 16:144 + k * 16, :]

    pl.semaphore_wait(
        barrier,
        (1 + has_x[1] + has_x[-1]) * (1 + has_y[1] + has_y[-1]) - 1,
    )

    def message(k):
        (dx, dy), (start, size) = WAYS[k], SLOTS[k]
        return pltpu.make_async_remote_copy(
            src_ref=out_buf.at[pl.ds(start, size)],
            dst_ref=in_buf.at[pl.ds(start, size)],
            send_sem=send_sem.at[k],
            recv_sem=recv_sem.at[k],
            device_id=(py + dy, px + dx),
            device_id_type=MESH,
        )

    order = (2, 3, 4, 5, 6, 7, 0, 1)
    for k in order:
        @pl.when(exists(*WAYS[k]))
        def _():
            message(k).start()

    own1 = dot(s1_v[144:, :], z1)
    own2 = dot(s2_v[192:, :], z2)
    loads[4].wait()
    loads[5].wait()

    for k in order:
        dx, dy = WAYS[k]

        @pl.when(exists(-dx, -dy))
        def _():
            message(k).wait_recv()

    halo1 = [
        jnp.concatenate(
            [in_buf[k * FACE:k * FACE + 32, :], in_buf[k * FACE + 32:k * FACE + 64, :]], axis=1
        )
        for k in range(4)
    ]
    halo2 = [in_buf[k * FACE + 64:k * FACE + 96, :] for k in range(4)]
    for k in range(4):
        at = 4 * FACE + k * CORNER
        halo1.append(jnp.concatenate([in_buf[at:at + 4, :], in_buf[at + 4:at + 8, :]], axis=1))
        halo2.append(in_buf[at + 8:at + 24, :])
    o2 = own2 + dot(u2_v[...], jnp.concatenate(halo2, axis=0))
    o1 = own1 + dot(u1_v[...], jnp.concatenate(halo1, axis=0))

    o2 = o2.reshape(4, 4, 8, 128)
    for band in range(4):
        for bz in range(2):
            part = o2[band, :, :4, bz * 64:bz * 64 + 64]
            if band + bz:
                two[2 * band + bz - 1] = part
                one[2 * band + bz - 1] = o1[
                    band * 64:band * 64 + 64, bz * 128:bz * 128 + 128
                ].reshape(8, 8, 128)
            else:
                approx[...] = part

    for k in order:
        @pl.when(exists(*WAYS[k]))
        def _():
            message(k).wait_send()


def store(approx_v, two_v, one_v, approx, two, one, sem):
    pairs = ((one_v, one), (two_v, two), (approx_v, approx))
    copies = [pltpu.make_async_copy(a, b, sem.at[k]) for k, (a, b) in enumerate(pairs)]
    for copy in copies:
        copy.start()
    for copy in copies:
        copy.wait()


def per_device(nx, ny, velocity):
    bx, by, nz = velocity.shape
    consts = matrices(bx, by, nz)
    f32 = jnp.float32
    vmem = pl.BlockSpec(memory_space=pltpu.VMEM)
    tables = [pltpu.VMEM(c.shape[-2:], f32) for c in consts]
    shapes = (
        (bx // 4, by // 4, nz // 4),
        (7, bx // 4, by // 4, nz // 4),
        (7, bx // 2, by // 2, nz // 2),
    )
    results = pl.pallas_call(
        functools.partial(kernel, nx, ny),
        out_shape=tuple(pltpu.VMEM(shape, f32) for shape in shapes),
        in_specs=[pl.BlockSpec(memory_space=pl.ANY)] * 6,
        out_specs=(vmem, vmem, vmem),
        scratch_shapes=[pltpu.VMEM((bx, by, nz), f32)]
        + tables
        + [
            pltpu.VMEM((4 * (FACE + CORNER), 128), f32),
            pltpu.VMEM((4 * (FACE + CORNER), 128), f32),
            pltpu.SemaphoreType.DMA((6,)),
            pltpu.SemaphoreType.DMA((8,)),
            pltpu.SemaphoreType.DMA((8,)),
        ],
        compiler_params=pltpu.CompilerParams(
            collective_id=0, has_side_effects=True, vmem_limit_bytes=60 * 1024 * 1024
        ),
    )(velocity, *[jnp.asarray(c) for c in consts])
    results = [pltpu.with_memory_space_constraint(r, pltpu.VMEM) for r in results]
    return pl.pallas_call(
        store,
        out_shape=tuple(jax.ShapeDtypeStruct(shape, f32) for shape in shapes),
        in_specs=[vmem] * 3,
        out_specs=[pl.BlockSpec(memory_space=pl.ANY)] * 3,
        scratch_shapes=[pltpu.SemaphoreType.DMA((3,))],
    )(*results)


def solution(mesh):
    placed = (P("slab", "morton", None),)
    return jax.shard_map(
        functools.partial(per_device, mesh.shape["slab"], mesh.shape["morton"]),
        mesh=mesh,
        in_specs=placed,
        out_specs=(
            P("slab", "morton", None),
            P(None, "slab", "morton", None),
            P(None, "slab", "morton", None),
        ),
        check_vma=False,
    )
```

```python
import functools

import jax
import jax.numpy as jnp
import numpy as np
from jax import lax
from jax.experimental import pallas as pl
from jax.experimental.pallas import tpu as pltpu
from jax.sharding import PartitionSpec as P

LIFT_ALPHA = -1.586134342059924
LIFT_BETA = -0.052980118572961
LIFT_GAMMA = 0.882911075530934
LIFT_DELTA = 0.443506852043971
LIFT_SCALE = 1.149604398860241

MESH = pl.DeviceIdType.MESH
FACES = ((1, 0), (-1, 0), (0, 1), (0, -1))
CORNERS = ((1, 1), (1, -1), (-1, 1), (-1, -1))
WAYS = FACES + CORNERS
ORDER = (2, 3, 4, 5, 6, 7, 0, 1)
HIGHEST = lax.Precision.HIGHEST


def lift_matrix(n):
    x = np.pad(np.eye(n), ((4, 4), (0, 0)), mode="reflect")
    e, o = x[0::2], x[1::2]
    d1 = o[:-1] + LIFT_ALPHA * (e[:-1] + e[1:])
    s1 = e[1:-1] + LIFT_BETA * (d1[:-1] + d1[1:])
    d2 = d1[1:-1] + LIFT_GAMMA * (s1[:-1] + s1[1:])
    s2 = s1[1:-1] + LIFT_DELTA * (d2[:-1] + d2[1:])
    return s2 * LIFT_SCALE, d2[1:] / LIFT_SCALE


def low_rank(coupling, rank):
    rest, us, vs = coupling.copy(), [], []
    for _ in range(rank):
        i, j = np.unravel_index(np.argmax(np.abs(rest)), rest.shape)
        u, v = rest[:, j] / rest[i, j], rest[i, :].copy()
        us.append(u)
        vs.append(v)
        rest = rest - u[:, None] * v[None, :]
    assert np.abs(rest).max() < 1e-12
    return np.stack(us, 1), np.stack(vs, 0)


def block_maps(b):
    blocks = 5
    low, high = lift_matrix(blocks * b)
    low2, high2 = lift_matrix(blocks * b // 2)
    pairs = ((low, high, 2), (low2 @ low, high2 @ low, 4))
    levels = []
    for lows, highs, rank in pairs:
        n = lows.shape[0] // blocks

        def part(row, col):
            cols = slice(col * b, (col + 1) * b)
            rows = slice(row * n, (row + 1) * n)
            return np.concatenate([lows[rows, cols], highs[rows, cols]])

        for row in range(blocks):
            for col in range(blocks):
                if abs(row - col) > 1:
                    assert np.abs(part(row, col)).max() == 0
                elif row != col:
                    like = part(2, 2 + col - row)
                    assert np.abs(part(row, col) - like).max() < 1e-12
        assert np.abs(part(1, 1) - part(2, 2)).max() < 1e-12
        assert np.abs(part(3, 3) - part(2, 2)).max() < 1e-12
        own = [part(0, 0), part(2, 2), part(4, 4)]
        u_up, v_up = low_rank(part(2, 1), rank)
        u_down, v_down = low_rank(part(2, 3), rank)
        levels.append((own, {1: u_up, -1: u_down}, {1: v_up, -1: v_down}))
    return levels


@functools.lru_cache(maxsize=None)
def matrices(bx, by, nz):
    low, high = lift_matrix(nz)
    low2, high2 = lift_matrix(nz // 2)
    depth1 = np.concatenate([low, high]).T.astype(np.float32)
    depth2 = np.concatenate([low2 @ low, high2 @ low]).T.astype(np.float32)
    sends, spreads = [], []
    for level, pad in ((0, 1), (1, 2)):
        own_x, ux, vx = block_maps(bx)[level]
        own_y, uy, vy = block_maps(by)[level]
        nx, ny = own_x[0].shape[0], own_y[0].shape[0]
        eye_x, eye_y = np.eye(nx), np.eye(ny)
        spread = [np.kron(ux[dx] if dx else eye_x, uy[dy] if dy else eye_y) for dx, dy in WAYS]

        def by_band(m):
            m = m.reshape(2, nx // 2, 2, ny // 2, -1).transpose(0, 2, 1, 3, 4)
            m = np.pad(m, ((0, 0),) * 3 + ((0, (pad - 1) * (ny // 2)), (0, 0)))
            return m.reshape(-1, m.shape[-1])

        spreads.append(by_band(np.concatenate(spread, 1)).astype(np.float32))
        rows = []
        for cx in range(3):
            for cy in range(3):
                out = [
                    np.kron(vx[dx] if dx else own_x[cx], vy[dy] if dy else own_y[cy])
                    for dx, dy in WAYS
                ]
                out.append(by_band(np.kron(own_x[cx], own_y[cy])))
                rows.append(np.concatenate(out))
        sends.append(np.stack(rows).astype(np.float32))
    return depth1, depth2, sends[0], sends[1], spreads[0], spreads[1]


def dot(a, b):
    return jnp.dot(a, b, precision=HIGHEST, preferred_element_type=jnp.float32)


def kernel(
    nx, ny, x_hbm, t1_hbm, t2_hbm, s1_hbm, s2_hbm, u1_hbm, u2_hbm, approx, two, one,
    x_v, t1_v, t2_v, s1_v, s2_v, u1_v, u2_v,
    face1_out, face1_in, corner1_out, corner1_in, out2, in2,
    load_sem, send1, recv1, send2, recv2,
):
    px, py = lax.axis_index("slab"), lax.axis_index("morton")
    not_first_x, last_x = lax.div(px + (nx - 2), nx - 1), lax.div(px, nx - 1)
    not_first_y, last_y = lax.div(py + (ny - 2), ny - 1), lax.div(py, ny - 1)
    here = (not_first_x + last_x) * 3 + not_first_y + last_y
    has_x = {1: 1 - last_x, -1: not_first_x, 0: 1}
    has_y = {1: 1 - last_y, -1: not_first_y, 0: 1}

    def exists(dx, dy):
        return has_x[dx] * has_y[dy] == 1

    def rows(ref, start, size):
        return ref.at[pl.ds(start, size)]

    n1, n2 = s1_v.shape[0] - 144, s2_v.shape[0] - 192
    loads = [
        pltpu.make_async_copy(source, target, load_sem.at[k])
        for k, (source, target) in enumerate((
            (x_hbm, x_v),
            (t1_hbm, t1_v),
            (s1_hbm.at[here, pl.ds(0, 144)], rows(s1_v, 0, 144)),
            (t2_hbm, t2_v),
            (s2_hbm.at[here, pl.ds(0, 192)], rows(s2_v, 0, 192)),
            (s1_hbm.at[here, pl.ds(144, n1)], rows(s1_v, 144, n1)),
            (s2_hbm.at[here, pl.ds(192, n2)], rows(s2_v, 192, n2)),
            (u1_hbm, u1_v),
            (u2_hbm, u2_v),
        ))
    ]
    for load in loads:
        load.start()

    barrier = pltpu.get_barrier_semaphore()
    for dx, dy in WAYS:
        @pl.when(exists(dx, dy))
        def _():
            pl.semaphore_signal(
                barrier, inc=1, device_id=(py + dy, px + dx), device_id_type=MESH
            )

    def message(level, k):
        dx, dy = WAYS[k]
        if level == 1 and k < 4:
            pair = rows(face1_out, k * 32, 32), rows(face1_in, k * 32, 32)
        elif level == 1:
            pair = corner1_out.at[k - 4], corner1_in.at[k - 4]
        elif k < 4:
            pair = rows(out2, k * 32, 32), rows(in2, k * 32, 32)
        else:
            pair = rows(out2, 64 + k * 16, 16), rows(in2, 64 + k * 16, 16)
        send, recv = (send1, recv1) if level == 1 else (send2, recv2)
        return pltpu.make_async_remote_copy(
            src_ref=pair[0],
            dst_ref=pair[1],
            send_sem=send.at[k],
            recv_sem=recv.at[k],
            device_id=(py + dy, px + dx),
            device_id_type=MESH,
        )

    def start(level):
        for k in ORDER:
            @pl.when(exists(*WAYS[k]))
            def _():
                message(level, k).start()

    def receive(level):
        for k in ORDER:
            dx, dy = WAYS[k]

            @pl.when(exists(-dx, -dy))
            def _():
                message(level, k).wait_recv()

    for k, (dx, dy) in enumerate(WAYS):
        @pl.when(jnp.logical_not(exists(-dx, -dy)))
        def _():
            if k < 4:
                face1_in[k * 32:k * 32 + 32, :] = jnp.zeros((32, 256), jnp.float32)
                in2[k * 32:k * 32 + 32, :] = jnp.zeros((32, 128), jnp.float32)
            else:
                corner1_in[k - 4] = jnp.zeros((4, 256), jnp.float32)
                in2[64 + k * 16:80 + k * 16, :] = jnp.zeros((16, 128), jnp.float32)

    loads[0].wait()
    loads[1].wait()
    x = x_v[...].reshape(256, 256)
    z1 = dot(x, t1_v[...])
    loads[2].wait()
    p1 = dot(s1_v[:144, :], z1)
    face1_out[...] = p1[:128, :]
    corner1_out[...] = p1[128:144, :].reshape(4, 4, 256)
    pl.semaphore_wait(
        barrier,
        (1 + has_x[1] + has_x[-1]) * (1 + has_y[1] + has_y[-1]) - 1,
    )
    start(1)

    loads[3].wait()
    z2 = dot(x, t2_v[...])
    loads[4].wait()
    out2[...] = dot(s2_v[:192, :], z2)
    start(2)

    for load in loads[5:]:
        load.wait()
    own1 = dot(s1_v[144:, :], z1)
    own2 = dot(s2_v[192:, :], z2)

    receive(1)
    halo1 = jnp.concatenate([face1_in[...], corner1_in[...].reshape(16, 256)], axis=0)
    o1 = own1 + dot(u1_v[...], halo1)
    for band in range(4):
        for bz in range(2):
            if band + bz:
                one[2 * band + bz - 1] = o1[
                    band * 64:band * 64 + 64, bz * 128:bz * 128 + 128
                ].reshape(8, 8, 128)

    receive(2)
    o2 = (own2 + dot(u2_v[...], in2[...])).reshape(4, 4, 8, 128)
    for band in range(4):
        for bz in range(2):
            part = o2[band, :, :4, bz * 64:bz * 64 + 64]
            if band + bz:
                two[2 * band + bz - 1] = part
            else:
                approx[...] = part

    for level in (1, 2):
        for k in ORDER:
            @pl.when(exists(*WAYS[k]))
            def _():
                message(level, k).wait_send()


def store(approx_v, two_v, one_v, approx, two, one, sem):
    pairs = ((one_v, one), (two_v, two), (approx_v, approx))
    copies = [pltpu.make_async_copy(a, b, sem.at[k]) for k, (a, b) in enumerate(pairs)]
    for copy in copies:
        copy.start()
    for copy in copies:
        copy.wait()


def per_device(nx, ny, velocity):
    bx, by, nz = velocity.shape
    consts = matrices(bx, by, nz)
    f32 = jnp.float32
    vmem = pl.BlockSpec(memory_space=pltpu.VMEM)
    tables = [pltpu.VMEM(c.shape[-2:], f32) for c in consts]
    shapes = (
        (bx // 4, by // 4, nz // 4),
        (7, bx // 4, by // 4, nz // 4),
        (7, bx // 2, by // 2, nz // 2),
    )
    results = pl.pallas_call(
        functools.partial(kernel, nx, ny),
        out_shape=tuple(pltpu.VMEM(shape, f32) for shape in shapes),
        in_specs=[pl.BlockSpec(memory_space=pl.ANY)] * 7,
        out_specs=(vmem, vmem, vmem),
        scratch_shapes=[pltpu.VMEM((bx, by, nz), f32)]
        + tables
        + [
            pltpu.VMEM((128, 256), f32),
            pltpu.VMEM((128, 256), f32),
            pltpu.VMEM((4, 4, 256), f32),
            pltpu.VMEM((4, 4, 256), f32),
            pltpu.VMEM((192, 128), f32),
            pltpu.VMEM((192, 128), f32),
            pltpu.SemaphoreType.DMA((9,)),
        ]
        + [pltpu.SemaphoreType.DMA((8,))] * 4,
        compiler_params=pltpu.CompilerParams(
            collective_id=0, has_side_effects=True, vmem_limit_bytes=60 * 1024 * 1024
        ),
    )(velocity, *[jnp.asarray(c) for c in consts])
    results = [pltpu.with_memory_space_constraint(r, pltpu.VMEM) for r in results]
    return pl.pallas_call(
        store,
        out_shape=tuple(jax.ShapeDtypeStruct(shape, f32) for shape in shapes),
        in_specs=[vmem] * 3,
        out_specs=[pl.BlockSpec(memory_space=pl.ANY)] * 3,
        scratch_shapes=[pltpu.SemaphoreType.DMA((3,))],
    )(*results)


def solution(mesh):
    placed = (P("slab", "morton", None),)
    return jax.shard_map(
        functools.partial(per_device, mesh.shape["slab"], mesh.shape["morton"]),
        mesh=mesh,
        in_specs=placed,
        out_specs=(
            P("slab", "morton", None),
            P(None, "slab", "morton", None),
            P(None, "slab", "morton", None),
        ),
        check_vma=False,
    )
```

```python
import functools

import jax
import jax.numpy as jnp
import numpy as np
from jax import lax
from jax.experimental import pallas as pl
from jax.experimental.pallas import tpu as pltpu
from jax.sharding import PartitionSpec as P

LIFT_ALPHA = -1.586134342059924
LIFT_BETA = -0.052980118572961
LIFT_GAMMA = 0.882911075530934
LIFT_DELTA = 0.443506852043971
LIFT_SCALE = 1.149604398860241

MESH = pl.DeviceIdType.MESH
FACES = ((1, 0), (-1, 0), (0, 1), (0, -1))
CORNERS = ((1, 1), (1, -1), (-1, 1), (-1, -1))
WAYS = FACES + CORNERS
ORDER = (2, 3, 4, 5, 6, 7, 0, 1)
HIGHEST = lax.Precision.HIGHEST


def lift_matrix(n):
    x = np.pad(np.eye(n), ((4, 4), (0, 0)), mode="reflect")
    e, o = x[0::2], x[1::2]
    d1 = o[:-1] + LIFT_ALPHA * (e[:-1] + e[1:])
    s1 = e[1:-1] + LIFT_BETA * (d1[:-1] + d1[1:])
    d2 = d1[1:-1] + LIFT_GAMMA * (s1[:-1] + s1[1:])
    s2 = s1[1:-1] + LIFT_DELTA * (d2[:-1] + d2[1:])
    return s2 * LIFT_SCALE, d2[1:] / LIFT_SCALE


def low_rank(coupling, rank):
    rest, us, vs = coupling.copy(), [], []
    for _ in range(rank):
        i, j = np.unravel_index(np.argmax(np.abs(rest)), rest.shape)
        u, v = rest[:, j] / rest[i, j], rest[i, :].copy()
        us.append(u)
        vs.append(v)
        rest = rest - u[:, None] * v[None, :]
    assert np.abs(rest).max() < 1e-12
    return np.stack(us, 1), np.stack(vs, 0)


def block_maps(b):
    blocks = 5
    low, high = lift_matrix(blocks * b)
    low2, high2 = lift_matrix(blocks * b // 2)
    pairs = ((low, high, 2), (low2 @ low, high2 @ low, 4))
    levels = []
    for lows, highs, rank in pairs:
        n = lows.shape[0] // blocks

        def part(row, col):
            cols = slice(col * b, (col + 1) * b)
            rows = slice(row * n, (row + 1) * n)
            return np.concatenate([lows[rows, cols], highs[rows, cols]])

        for row in range(blocks):
            for col in range(blocks):
                if abs(row - col) > 1:
                    assert np.abs(part(row, col)).max() == 0
                elif row != col:
                    like = part(2, 2 + col - row)
                    assert np.abs(part(row, col) - like).max() < 1e-12
        assert np.abs(part(1, 1) - part(2, 2)).max() < 1e-12
        assert np.abs(part(3, 3) - part(2, 2)).max() < 1e-12
        own = [part(0, 0), part(2, 2), part(4, 4)]
        u_up, v_up = low_rank(part(2, 1), rank)
        u_down, v_down = low_rank(part(2, 3), rank)
        levels.append((own, {1: u_up, -1: u_down}, {1: v_up, -1: v_down}))
    return levels


@functools.lru_cache(maxsize=None)
def tables(bx, by, nz):
    low, high = lift_matrix(nz)
    low2, high2 = lift_matrix(nz // 2)
    depth1 = np.concatenate([low, high]).T
    depth2 = np.concatenate([low2, high2]).T
    levels_x, levels_y = block_maps(bx), block_maps(by)
    own_x, ux, vx = levels_x[1]
    own_y, uy, vy = levels_y[1]
    nx, ny = own_x[0].shape[0], own_y[0].shape[0]
    plane = []
    for cx in range(3):
        for cy in range(3):
            out = []
            for dx, dy in WAYS:
                m = np.kron(vx[dx] if dx else own_x[cx], vy[dy] if dy else own_y[cy])
                if dx == 0:
                    m = m.reshape(nx, -1, bx * by).transpose(1, 0, 2).reshape(-1, bx * by)
                out.append(m)
            out.append(np.kron(own_x[cx], own_y[cy]))
            plane.append(np.concatenate(out))
    columns = np.concatenate([u[d].T.reshape(-1) for u in (levels_y[0][1], uy) for d in (1, -1)])
    columns = np.repeat(columns[:, None], 128, axis=1)
    arrays = [t.astype(np.float32) for t in (depth1, depth2, np.stack(plane), columns)]
    return arrays, levels_x, levels_y


def dot(a, b):
    return jnp.dot(a, b, precision=HIGHEST, preferred_element_type=jnp.float32)


def lift_ends(e, o, prev, after, first, last):
    at, sub = jnp.where, lambda f, *lists: [f(*v) for v in zip(*lists)]
    e_after = after(e, sub(lambda p: at(last, p, 0.0), e))
    d1 = sub(lambda p, q, r: p + LIFT_ALPHA * (q + r), o, e, e_after)
    out1 = sub(lambda p: LIFT_ALPHA * p, e)
    d1_prev = prev(d1, sub(lambda p, q: at(first, p, q), d1, out1))
    s1 = sub(lambda p, q, r: p + LIFT_BETA * (q + r), e, d1_prev, d1)
    s1_after = after(s1, sub(lambda p, q: at(last, p, LIFT_BETA * q), s1, d1))
    d2 = sub(lambda p, q, r: p + LIFT_GAMMA * (q + r), d1, s1, s1_after)
    out2 = sub(lambda p, q: p + LIFT_GAMMA * (LIFT_BETA * p + q), out1, s1)
    d2_prev = prev(d2, sub(lambda p, q: at(first, p, q), d2, out2))
    s2 = sub(lambda p, q, r: p + LIFT_DELTA * (q + r), s1, d2_prev, d2)
    return [v * LIFT_SCALE for v in s2], [v * (1.0 / LIFT_SCALE) for v in d2]


def weighted(weights, values):
    terms = [float(w) * v for w, v in zip(weights, values) if w != 0.0]
    return functools.reduce(lambda p, q: p + q, terms)


def kernel(
    nx, ny, levels_x, levels_y, x_hbm, t1_hbm, t2_hbm, s2_hbm, uy_hbm, approx, two, one,
    x_v, t1_v, t2_v, s2_v, uy_v, xb, own1,
    face1_out, face1_in, corner1_out, corner1_in, out2, in2,
    load_sem, send1, recv1, send2, recv2,
):
    px, py = lax.axis_index("slab"), lax.axis_index("morton")
    not_first_x, last_x = lax.div(px + (nx - 2), nx - 1), lax.div(px, nx - 1)
    not_first_y, last_y = lax.div(py + (ny - 2), ny - 1), lax.div(py, ny - 1)
    here = (not_first_x + last_x) * 3 + not_first_y + last_y
    has_x = {1: 1 - last_x, -1: not_first_x, 0: 1}
    has_y = {1: 1 - last_y, -1: not_first_y, 0: 1}

    def exists(dx, dy):
        return has_x[dx] * has_y[dy] == 1

    def rows(ref, start, size):
        return ref.at[pl.ds(start, size)]

    loads = [
        pltpu.make_async_copy(source, target, load_sem.at[k])
        for k, (source, target) in enumerate((
            (x_hbm, x_v),
            (t1_hbm, t1_v),
            (t2_hbm, t2_v),
            (s2_hbm.at[here], s2_v),
            (uy_hbm, uy_v),
        ))
    ]
    for load in loads:
        load.start()

    barrier = pltpu.get_barrier_semaphore()
    for dx, dy in WAYS:
        @pl.when(exists(dx, dy))
        def _():
            pl.semaphore_signal(
                barrier, inc=1, device_id=(py + dy, px + dx), device_id_type=MESH
            )

    def message(level, k):
        dx, dy = WAYS[k]
        if level == 1 and k < 4:
            pair = rows(face1_out, k * 32, 32), rows(face1_in, k * 32, 32)
        elif level == 1:
            pair = corner1_out.at[k - 4], corner1_in.at[k - 4]
        elif k < 4:
            pair = rows(out2, k * 32, 32), rows(in2, k * 32, 32)
        else:
            pair = rows(out2, 64 + k * 16, 16), rows(in2, 64 + k * 16, 16)
        send, recv = (send1, recv1) if level == 1 else (send2, recv2)
        return pltpu.make_async_remote_copy(
            src_ref=pair[0],
            dst_ref=pair[1],
            send_sem=send.at[k],
            recv_sem=recv.at[k],
            device_id=(py + dy, px + dx),
            device_id_type=MESH,
        )

    def start(level):
        for k in ORDER:
            @pl.when(exists(*WAYS[k]))
            def _():
                message(level, k).start()

    def receive(level):
        for k in ORDER:
            dx, dy = WAYS[k]

            @pl.when(exists(-dx, -dy))
            def _():
                message(level, k).wait_recv()

    for k, (dx, dy) in enumerate(WAYS):
        @pl.when(jnp.logical_not(exists(-dx, -dy)))
        def _():
            if k < 4:
                face1_in[k * 32:k * 32 + 32, :] = jnp.zeros((32, 256), jnp.float32)
                in2[k * 32:k * 32 + 32, :] = jnp.zeros((32, 128), jnp.float32)
            else:
                corner1_in[k - 4] = jnp.zeros((4, 256), jnp.float32)
                in2[64 + k * 16:80 + k * 16, :] = jnp.zeros((16, 128), jnp.float32)

    loads[0].wait()
    loads[1].wait()
    z1 = dot(x_v[...].reshape(256, 256), t1_v[...])

    planes = [z1[16 * i:16 * i + 16, :] for i in range(16)]
    low, high = lift_ends(
        planes[0::2], planes[1::2],
        lambda v, end: [end[0]] + v[:-1],
        lambda v, end: v[1:] + [end[-1]],
        not_first_x == 0, last_x == 1,
    )
    _, ux, vx = levels_x[0]
    _, uy, vy = levels_y[0]
    along = [weighted(w, planes) for d in (1, -1) for w in vx[d]]
    for r, v in enumerate(low + high + along):
        for h in range(2):
            xb[320 * h + 16 * r:320 * h + 16 * r + 16, :] = v[:, 128 * h:128 * h + 128]

    def strided(begin, size, stride):
        return jnp.concatenate(
            [xb[pl.ds(320 * h + begin, size, stride=stride), :] for h in range(2)], axis=1
        )

    for kd, d in enumerate((1, -1)):
        for ky in range(2):
            taps = [y for y in range(16) if vy[d][ky, y] != 0.0]
            weights = [vy[d][ky, y] for y in taps]
            at = (2 + kd) * 32 + ky * 16
            face1_out[at:at + 16, :] = weighted(
                weights, [strided(y, 16, 16) for y in taps]
            )
            part = weighted(weights, [strided(256 + y, 4, 16) for y in taps])
            corner1_out[kd, 2 * ky:2 * ky + 2, :] = part[0:2]
            corner1_out[2 + kd, 2 * ky:2 * ky + 2, :] = part[2:4]

    place = lax.broadcasted_iota(jnp.int32, (8, 256), 0)
    for r in (16, 17, 18, 19) + tuple(range(16)):
        low, high = lift_ends(
            [strided(16 * r, 8, 2)], [strided(16 * r + 1, 8, 2)],
            lambda v, end: [jnp.where(place == 0, end[0], pltpu.roll(v[0], 1, 0))],
            lambda v, end: [jnp.where(place == 7, end[0], pltpu.roll(v[0], 7, 0))],
            not_first_y == 0, last_y == 1,
        )
        if r >= 16:
            at = (r - 16) * 16
            face1_out[at:at + 8, :] = low[0]
            face1_out[at + 8:at + 16, :] = high[0]
        else:
            own1[r, 0] = low[0]
            own1[r, 1] = high[0]
        if r == 19:
            pl.semaphore_wait(
                barrier,
                (1 + has_x[1] + has_x[-1]) * (1 + has_y[1] + has_y[-1]) - 1,
            )
            start(1)

    loads[2].wait()
    z2 = dot(z1[:, :128], t2_v[...])
    loads[3].wait()
    p2 = dot(s2_v[...], z2)
    out2[...] = p2[:192, :]
    start(2)
    own2 = p2[192:, :]
    loads[4].wait()

    receive(1)
    for bz in range(2):
        half = slice(bz * 128, bz * 128 + 128)
        column = [[[
            uy_v[((kd * 2 + ky) * 2 + b) * 8:((kd * 2 + ky) * 2 + b) * 8 + 8, :]
            for b in range(2)] for ky in range(2)] for kd in range(2)]

        def add_y(value, row, b):
            for kd in range(2):
                for ky in range(2):
                    value = value + row(kd, ky) * column[kd][ky][b]
            return value

        for b in range(2):
            side = [
                [
                    add_y(
                        face1_in[dx * 32 + kx * 16 + b * 8:dx * 32 + kx * 16 + b * 8 + 8, half],
                        lambda kd, ky: corner1_in[dx * 2 + kd, 2 * ky + kx:2 * ky + kx + 1, half],
                        b,
                    )
                    for kx in range(2)
                ]
                for dx in range(2)
            ]
            for r in range(16):
                band, i = 2 * (r // 8) + b, r % 8
                if band + bz == 0:
                    continue
                value = add_y(
                    own1[r, b, :, half],
                    lambda kd, ky: face1_in[
                        (2 + kd) * 32 + ky * 16 + r:(2 + kd) * 32 + ky * 16 + r + 1, half
                    ],
                    b,
                )
                for dx, d in enumerate((1, -1)):
                    if np.any(ux[d][r] != 0.0):
                        value = value + weighted(ux[d][r], side[dx])
                one[2 * band + bz - 1, i] = value

    receive(2)
    _, ux2, _ = levels_x[1]
    column2 = [uy_v[64 + k * 8:72 + k * 8, :] for k in range(8)]
    side2 = [
        [
            in2[dx * 32 + kx * 8:dx * 32 + kx * 8 + 8, :]
            + sum(
                in2[at:at + 1, :] * column2[kd * 4 + ky]
                for kd in range(2)
                for ky in range(4)
                for at in (128 + (dx * 2 + kd) * 16 + kx * 4 + ky,)
            )
            for kx in range(4)
        ]
        for dx in range(2)
    ]
    for r in range(8):
        value = own2[r * 8:r * 8 + 8, :] + sum(
            in2[at:at + 1, :] * column2[kd * 4 + ky]
            for kd in range(2)
            for ky in range(4)
            for at in ((2 + kd) * 32 + ky * 8 + r,)
        )
        for dx, d in enumerate((1, -1)):
            if np.any(ux2[d][r] != 0.0):
                value = value + weighted(ux2[d][r], side2[dx])
        for b in range(2):
            for bz in range(2):
                at, part = 4 * (r // 4) + 2 * b + bz, value[4 * b:4 * b + 4, 64 * bz:64 * bz + 64]
                if at:
                    two[at - 1, r % 4] = part
                else:
                    approx[r % 4] = part

    for level in (1, 2):
        for k in ORDER:
            @pl.when(exists(*WAYS[k]))
            def _():
                message(level, k).wait_send()


def store(approx_v, two_v, one_v, approx, two, one, sem):
    pairs = ((one_v, one), (two_v, two), (approx_v, approx))
    copies = [pltpu.make_async_copy(a, b, sem.at[k]) for k, (a, b) in enumerate(pairs)]
    for copy in copies:
        copy.start()
    for copy in copies:
        copy.wait()


def per_device(nx, ny, velocity):
    bx, by, nz = velocity.shape
    consts, levels_x, levels_y = tables(bx, by, nz)
    f32 = jnp.float32
    vmem = pl.BlockSpec(memory_space=pltpu.VMEM)
    held = [pltpu.VMEM(c.shape[-2:], f32) for c in consts]
    shapes = (
        (bx // 4, by // 4, nz // 4),
        (7, bx // 4, by // 4, nz // 4),
        (7, bx // 2, by // 2, nz // 2),
    )
    results = pl.pallas_call(
        functools.partial(kernel, nx, ny, levels_x, levels_y),
        out_shape=tuple(pltpu.VMEM(shape, f32) for shape in shapes),
        in_specs=[pl.BlockSpec(memory_space=pl.ANY)] * 5,
        out_specs=(vmem, vmem, vmem),
        scratch_shapes=[pltpu.VMEM((bx, by, nz), f32)]
        + held
        + [
            pltpu.VMEM((640, 128), f32),
            pltpu.VMEM((16, 2, 8, 256), f32),
            pltpu.VMEM((128, 256), f32),
            pltpu.VMEM((128, 256), f32),
            pltpu.VMEM((4, 4, 256), f32),
            pltpu.VMEM((4, 4, 256), f32),
            pltpu.VMEM((192, 128), f32),
            pltpu.VMEM((192, 128), f32),
            pltpu.SemaphoreType.DMA((5,)),
        ]
        + [pltpu.SemaphoreType.DMA((8,))] * 4,
        compiler_params=pltpu.CompilerParams(
            collective_id=0, has_side_effects=True, vmem_limit_bytes=60 * 1024 * 1024
        ),
    )(velocity, *[jnp.asarray(c) for c in consts])
    results = [pltpu.with_memory_space_constraint(r, pltpu.VMEM) for r in results]
    return pl.pallas_call(
        store,
        out_shape=tuple(jax.ShapeDtypeStruct(shape, f32) for shape in shapes),
        in_specs=[vmem] * 3,
        out_specs=[pl.BlockSpec(memory_space=pl.ANY)] * 3,
        scratch_shapes=[pltpu.SemaphoreType.DMA((3,))],
    )(*results)


def solution(mesh):
    placed = (P("slab", "morton", None),)
    return jax.shard_map(
        functools.partial(per_device, mesh.shape["slab"], mesh.shape["morton"]),
        mesh=mesh,
        in_specs=placed,
        out_specs=(
            P("slab", "morton", None),
            P(None, "slab", "morton", None),
            P(None, "slab", "morton", None),
        ),
        check_vma=False,
    )
```

```python
import functools

import jax
import jax.numpy as jnp
import numpy as np
from jax import lax
from jax.experimental import pallas as pl
from jax.experimental.pallas import tpu as pltpu
from jax.sharding import PartitionSpec as P

LIFT_ALPHA = -1.586134342059924
LIFT_BETA = -0.052980118572961
LIFT_GAMMA = 0.882911075530934
LIFT_DELTA = 0.443506852043971
LIFT_SCALE = 1.149604398860241

MESH = pl.DeviceIdType.MESH
FACES = ((1, 0), (-1, 0), (0, 1), (0, -1))
CORNERS = ((1, 1), (1, -1), (-1, 1), (-1, -1))
WAYS = FACES + CORNERS
ORDER = (4, 5, 6, 7, 0, 1, 2, 3)
HIGHEST = lax.Precision.HIGHEST


def lift_matrix(n):
    x = np.pad(np.eye(n), ((4, 4), (0, 0)), mode="reflect")
    e, o = x[0::2], x[1::2]
    d1 = o[:-1] + LIFT_ALPHA * (e[:-1] + e[1:])
    s1 = e[1:-1] + LIFT_BETA * (d1[:-1] + d1[1:])
    d2 = d1[1:-1] + LIFT_GAMMA * (s1[:-1] + s1[1:])
    s2 = s1[1:-1] + LIFT_DELTA * (d2[:-1] + d2[1:])
    return s2 * LIFT_SCALE, d2[1:] / LIFT_SCALE


def low_rank(coupling, rank):
    rest, us, vs = coupling.copy(), [], []
    for _ in range(rank):
        i, j = np.unravel_index(np.argmax(np.abs(rest)), rest.shape)
        u, v = rest[:, j] / rest[i, j], rest[i, :].copy()
        us.append(u)
        vs.append(v)
        rest = rest - u[:, None] * v[None, :]
    assert np.abs(rest).max() < 1e-12
    return np.stack(us, 1), np.stack(vs, 0)


def block_maps(b):
    blocks = 5
    low, high = lift_matrix(blocks * b)
    low2, high2 = lift_matrix(blocks * b // 2)
    pairs = ((low, high, 2), (low2 @ low, high2 @ low, 4))
    levels = []
    for lows, highs, rank in pairs:
        n = lows.shape[0] // blocks

        def part(row, col):
            cols = slice(col * b, (col + 1) * b)
            rows = slice(row * n, (row + 1) * n)
            return np.concatenate([lows[rows, cols], highs[rows, cols]])

        for row in range(blocks):
            for col in range(blocks):
                if abs(row - col) > 1:
                    assert np.abs(part(row, col)).max() == 0
                elif row != col:
                    like = part(2, 2 + col - row)
                    assert np.abs(part(row, col) - like).max() < 1e-12
        assert np.abs(part(1, 1) - part(2, 2)).max() < 1e-12
        assert np.abs(part(3, 3) - part(2, 2)).max() < 1e-12
        own = [part(0, 0), part(2, 2), part(4, 4)]
        u_up, v_up = low_rank(part(2, 1), rank)
        u_down, v_down = low_rank(part(2, 3), rank)
        levels.append((own, {1: u_up, -1: u_down}, {1: v_up, -1: v_down}))
    return levels


@functools.lru_cache(maxsize=None)
def tables(bx, by, nz):
    low, high = lift_matrix(nz)
    low2, high2 = lift_matrix(nz // 2)
    depth1 = np.concatenate([low, high]).T
    depth2 = np.concatenate([low2, high2]).T
    levels_x, levels_y = block_maps(bx), block_maps(by)
    own_x, ux, vx = levels_x[1]
    own_y, uy, vy = levels_y[1]
    nx, ny = own_x[0].shape[0], own_y[0].shape[0]
    plane = []
    for cx in range(3):
        for cy in range(3):
            out = []
            for dx, dy in WAYS:
                m = np.kron(vx[dx] if dx else own_x[cx], vy[dy] if dy else own_y[cy])
                if dx == 0:
                    m = m.reshape(nx, -1, bx * by).transpose(1, 0, 2).reshape(-1, bx * by)
                out.append(m)
            out.append(np.kron(own_x[cx], own_y[cy]))
            plane.append(np.concatenate(out))
    columns = np.concatenate([u[d].T.reshape(-1) for u in (levels_y[0][1], uy) for d in (1, -1)])
    columns = np.repeat(columns[:, None], 128, axis=1)
    arrays = [t.astype(np.float32) for t in (depth1, depth2, np.stack(plane), columns)]
    return arrays, levels_x, levels_y


def dot(a, b):
    return jnp.dot(a, b, precision=HIGHEST, preferred_element_type=jnp.float32)


def lift_ends(e, o, prev, after, first, last):
    at, sub = jnp.where, lambda f, *lists: [f(*v) for v in zip(*lists)]
    e_after = after(e, sub(lambda p: at(last, p, 0.0), e))
    d1 = sub(lambda p, q, r: p + LIFT_ALPHA * (q + r), o, e, e_after)
    out1 = sub(lambda p: LIFT_ALPHA * p, e)
    d1_prev = prev(d1, sub(lambda p, q: at(first, p, q), d1, out1))
    s1 = sub(lambda p, q, r: p + LIFT_BETA * (q + r), e, d1_prev, d1)
    s1_after = after(s1, sub(lambda p, q: at(last, p, LIFT_BETA * q), s1, d1))
    d2 = sub(lambda p, q, r: p + LIFT_GAMMA * (q + r), d1, s1, s1_after)
    out2 = sub(lambda p, q: p + LIFT_GAMMA * (LIFT_BETA * p + q), out1, s1)
    d2_prev = prev(d2, sub(lambda p, q: at(first, p, q), d2, out2))
    s2 = sub(lambda p, q, r: p + LIFT_DELTA * (q + r), s1, d2_prev, d2)
    return [v * LIFT_SCALE for v in s2], [v * (1.0 / LIFT_SCALE) for v in d2]


def weighted(weights, values):
    terms = [float(w) * v for w, v in zip(weights, values) if w != 0.0]
    return functools.reduce(lambda p, q: p + q, terms)


def kernel(
    nx, ny, levels_x, levels_y, x_hbm, t1_hbm, t2_hbm, s2_hbm, uy_hbm, approx, two, one,
    x_v, t1_v, t2_v, s2_v, uy_v, xb, own1,
    face1_out, face1_in, corner1_out, corner1_in, out2, in2,
    load_sem, send1, recv1, send2, recv2,
):
    px, py = lax.axis_index("slab"), lax.axis_index("morton")
    not_first_x, last_x = lax.div(px + (nx - 2), nx - 1), lax.div(px, nx - 1)
    not_first_y, last_y = lax.div(py + (ny - 2), ny - 1), lax.div(py, ny - 1)
    here = (not_first_x + last_x) * 3 + not_first_y + last_y
    has_x = {1: 1 - last_x, -1: not_first_x, 0: 1}
    has_y = {1: 1 - last_y, -1: not_first_y, 0: 1}

    def exists(dx, dy):
        return has_x[dx] * has_y[dy] == 1

    def rows(ref, start, size):
        return ref.at[pl.ds(start, size)]

    loads = [
        pltpu.make_async_copy(source, target, load_sem.at[k])
        for k, (source, target) in enumerate((
            (x_hbm, x_v),
            (t1_hbm, t1_v),
            (t2_hbm, t2_v),
            (s2_hbm.at[here], s2_v),
            (uy_hbm, uy_v),
        ))
    ]
    for load in loads:
        load.start()

    barrier = pltpu.get_barrier_semaphore()
    for dx, dy in WAYS:
        @pl.when(exists(dx, dy))
        def _():
            pl.semaphore_signal(
                barrier, inc=1, device_id=(py + dy, px + dx), device_id_type=MESH
            )

    def message(level, k):
        dx, dy = WAYS[k]
        if level == 1 and k < 4:
            pair = rows(face1_out, k * 32, 32), rows(face1_in, k * 32, 32)
        elif level == 1:
            pair = corner1_out.at[k - 4], corner1_in.at[k - 4]
        elif k < 4:
            pair = rows(out2, k * 32, 32), rows(in2, k * 32, 32)
        else:
            pair = rows(out2, 64 + k * 16, 16), rows(in2, 64 + k * 16, 16)
        send, recv = (send1, recv1) if level == 1 else (send2, recv2)
        return pltpu.make_async_remote_copy(
            src_ref=pair[0],
            dst_ref=pair[1],
            send_sem=send.at[k],
            recv_sem=recv.at[k],
            device_id=(py + dy, px + dx),
            device_id_type=MESH,
        )

    def start(level):
        for k in ORDER:
            @pl.when(exists(*WAYS[k]))
            def _():
                message(level, k).start()

    def receive(level):
        for k in ORDER:
            dx, dy = WAYS[k]

            @pl.when(exists(-dx, -dy))
            def _():
                message(level, k).wait_recv()

    for k, (dx, dy) in enumerate(WAYS):
        @pl.when(jnp.logical_not(exists(-dx, -dy)))
        def _():
            if k < 4:
                face1_in[k * 32:k * 32 + 32, :] = jnp.zeros((32, 256), jnp.float32)
                in2[k * 32:k * 32 + 32, :] = jnp.zeros((32, 128), jnp.float32)
            else:
                corner1_in[k - 4] = jnp.zeros((4, 256), jnp.float32)
                in2[64 + k * 16:80 + k * 16, :] = jnp.zeros((16, 128), jnp.float32)

    loads[0].wait()
    loads[1].wait()
    z1 = dot(x_v[...].reshape(256, 256), t1_v[...])
    for load in loads[2:]:
        load.wait()
    z2 = dot(z1[:, :128], t2_v[...])
    p2 = dot(s2_v[...], z2)

    planes = [z1[16 * i:16 * i + 16, :] for i in range(16)]
    low, high = lift_ends(
        planes[0::2], planes[1::2],
        lambda v, end: [end[0]] + v[:-1],
        lambda v, end: v[1:] + [end[-1]],
        not_first_x == 0, last_x == 1,
    )
    _, ux, vx = levels_x[0]
    _, uy, vy = levels_y[0]
    along = [weighted(w, planes) for d in (1, -1) for w in vx[d]]
    for r, v in enumerate(low + high + along):
        for h in range(2):
            xb[320 * h + 16 * r:320 * h + 16 * r + 16, :] = v[:, 128 * h:128 * h + 128]

    def strided(begin, size, stride):
        return jnp.concatenate(
            [xb[pl.ds(320 * h + begin, size, stride=stride), :] for h in range(2)], axis=1
        )

    for kd, d in enumerate((1, -1)):
        for ky in range(2):
            taps = [y for y in range(16) if vy[d][ky, y] != 0.0]
            weights = [vy[d][ky, y] for y in taps]
            at = (2 + kd) * 32 + ky * 16
            face1_out[at:at + 16, :] = weighted(
                weights, [strided(y, 16, 16) for y in taps]
            )
            part = weighted(weights, [strided(256 + y, 4, 16) for y in taps])
            corner1_out[kd, 2 * ky:2 * ky + 2, :] = part[0:2]
            corner1_out[2 + kd, 2 * ky:2 * ky + 2, :] = part[2:4]

    place = lax.broadcasted_iota(jnp.int32, (8, 256), 0)
    for r in (16, 17, 18, 19) + tuple(range(16)):
        low, high = lift_ends(
            [strided(16 * r, 8, 2)], [strided(16 * r + 1, 8, 2)],
            lambda v, end: [jnp.where(place == 0, end[0], pltpu.roll(v[0], 1, 0))],
            lambda v, end: [jnp.where(place == 7, end[0], pltpu.roll(v[0], 7, 0))],
            not_first_y == 0, last_y == 1,
        )
        if r >= 16:
            at = (r - 16) * 16
            face1_out[at:at + 8, :] = low[0]
            face1_out[at + 8:at + 16, :] = high[0]
        else:
            own1[r, 0] = low[0]
            own1[r, 1] = high[0]

    out2[...] = p2[:192, :]
    own2 = p2[192:, :]
    pl.semaphore_wait(
        barrier,
        (1 + has_x[1] + has_x[-1]) * (1 + has_y[1] + has_y[-1]) - 1,
    )
    start(1)
    start(2)

    receive(1)
    for bz in range(2):
        half = slice(bz * 128, bz * 128 + 128)
        column = [[[
            uy_v[((kd * 2 + ky) * 2 + b) * 8:((kd * 2 + ky) * 2 + b) * 8 + 8, :]
            for b in range(2)] for ky in range(2)] for kd in range(2)]

        def add_y(value, row, b):
            for kd in range(2):
                for ky in range(2):
                    value = value + row(kd, ky) * column[kd][ky][b]
            return value

        for b in range(2):
            side = [
                [
                    add_y(
                        face1_in[dx * 32 + kx * 16 + b * 8:dx * 32 + kx * 16 + b * 8 + 8, half],
                        lambda kd, ky: corner1_in[dx * 2 + kd, 2 * ky + kx:2 * ky + kx + 1, half],
                        b,
                    )
                    for kx in range(2)
                ]
                for dx in range(2)
            ]
            for r in range(16):
                band, i = 2 * (r // 8) + b, r % 8
                if band + bz == 0:
                    continue
                value = add_y(
                    own1[r, b, :, half],
                    lambda kd, ky: face1_in[
                        (2 + kd) * 32 + ky * 16 + r:(2 + kd) * 32 + ky * 16 + r + 1, half
                    ],
                    b,
                )
                for dx, d in enumerate((1, -1)):
                    if np.any(ux[d][r] != 0.0):
                        value = value + weighted(ux[d][r], side[dx])
                one[2 * band + bz - 1, i] = value

    receive(2)
    _, ux2, _ = levels_x[1]
    column2 = [uy_v[64 + k * 8:72 + k * 8, :] for k in range(8)]
    side2 = [
        [
            in2[dx * 32 + kx * 8:dx * 32 + kx * 8 + 8, :]
            + sum(
                in2[at:at + 1, :] * column2[kd * 4 + ky]
                for kd in range(2)
                for ky in range(4)
                for at in (128 + (dx * 2 + kd) * 16 + kx * 4 + ky,)
            )
            for kx in range(4)
        ]
        for dx in range(2)
    ]
    for r in range(8):
        value = own2[r * 8:r * 8 + 8, :] + sum(
            in2[at:at + 1, :] * column2[kd * 4 + ky]
            for kd in range(2)
            for ky in range(4)
            for at in ((2 + kd) * 32 + ky * 8 + r,)
        )
        for dx, d in enumerate((1, -1)):
            if np.any(ux2[d][r] != 0.0):
                value = value + weighted(ux2[d][r], side2[dx])
        for b in range(2):
            for bz in range(2):
                at, part = 4 * (r // 4) + 2 * b + bz, value[4 * b:4 * b + 4, 64 * bz:64 * bz + 64]
                if at:
                    two[at - 1, r % 4] = part
                else:
                    approx[r % 4] = part

    for level in (1, 2):
        for k in ORDER:
            @pl.when(exists(*WAYS[k]))
            def _():
                message(level, k).wait_send()


def store(approx_v, two_v, one_v, approx, two, one, sem):
    pairs = [(one_v.at[k], one.at[k]) for k in range(7)] + [(two_v, two), (approx_v, approx)]
    copies = [pltpu.make_async_copy(a, b, sem.at[k]) for k, (a, b) in enumerate(pairs)]
    for copy in copies:
        copy.start()
    for copy in copies:
        copy.wait()


def per_device(nx, ny, velocity):
    bx, by, nz = velocity.shape
    consts, levels_x, levels_y = tables(bx, by, nz)
    f32 = jnp.float32
    vmem = pl.BlockSpec(memory_space=pltpu.VMEM)
    held = [pltpu.VMEM(c.shape[-2:], f32) for c in consts]
    shapes = (
        (bx // 4, by // 4, nz // 4),
        (7, bx // 4, by // 4, nz // 4),
        (7, bx // 2, by // 2, nz // 2),
    )
    results = pl.pallas_call(
        functools.partial(kernel, nx, ny, levels_x, levels_y),
        out_shape=tuple(pltpu.VMEM(shape, f32) for shape in shapes),
        in_specs=[pl.BlockSpec(memory_space=pl.ANY)] * 5,
        out_specs=(vmem, vmem, vmem),
        scratch_shapes=[pltpu.VMEM((bx, by, nz), f32)]
        + held
        + [
            pltpu.VMEM((640, 128), f32),
            pltpu.VMEM((16, 2, 8, 256), f32),
            pltpu.VMEM((128, 256), f32),
            pltpu.VMEM((128, 256), f32),
            pltpu.VMEM((4, 4, 256), f32),
            pltpu.VMEM((4, 4, 256), f32),
            pltpu.VMEM((192, 128), f32),
            pltpu.VMEM((192, 128), f32),
            pltpu.SemaphoreType.DMA((5,)),
        ]
        + [pltpu.SemaphoreType.DMA((8,))] * 4,
        compiler_params=pltpu.CompilerParams(
            collective_id=0, has_side_effects=True, vmem_limit_bytes=60 * 1024 * 1024
        ),
    )(velocity, *[jnp.asarray(c) for c in consts])
    results = [pltpu.with_memory_space_constraint(r, pltpu.VMEM) for r in results]
    return pl.pallas_call(
        store,
        out_shape=tuple(jax.ShapeDtypeStruct(shape, f32) for shape in shapes),
        in_specs=[vmem] * 3,
        out_specs=[pl.BlockSpec(memory_space=pl.ANY)] * 3,
        scratch_shapes=[pltpu.SemaphoreType.DMA((9,))],
    )(*results)


def solution(mesh):
    placed = (P("slab", "morton", None),)
    return jax.shard_map(
        functools.partial(per_device, mesh.shape["slab"], mesh.shape["morton"]),
        mesh=mesh,
        in_specs=placed,
        out_specs=(
            P("slab", "morton", None),
            P(None, "slab", "morton", None),
            P(None, "slab", "morton", None),
        ),
        check_vma=False,
    )
```

```python
import functools

import jax
import jax.numpy as jnp
import numpy as np
from jax import lax
from jax.experimental import pallas as pl
from jax.experimental.pallas import tpu as pltpu
from jax.sharding import PartitionSpec as P

LIFT_ALPHA = -1.586134342059924
LIFT_BETA = -0.052980118572961
LIFT_GAMMA = 0.882911075530934
LIFT_DELTA = 0.443506852043971
LIFT_SCALE = 1.149604398860241

MESH = pl.DeviceIdType.MESH
FACES = ((1, 0), (-1, 0), (0, 1), (0, -1))
CORNERS = ((1, 1), (1, -1), (-1, 1), (-1, -1))
WAYS = FACES + CORNERS
ORDER = (7, 3, 5, 1, 6, 0, 2, 4)
HIGHEST = lax.Precision.HIGHEST


def lift_matrix(n):
    x = np.pad(np.eye(n), ((4, 4), (0, 0)), mode="reflect")
    e, o = x[0::2], x[1::2]
    d1 = o[:-1] + LIFT_ALPHA * (e[:-1] + e[1:])
    s1 = e[1:-1] + LIFT_BETA * (d1[:-1] + d1[1:])
    d2 = d1[1:-1] + LIFT_GAMMA * (s1[:-1] + s1[1:])
    s2 = s1[1:-1] + LIFT_DELTA * (d2[:-1] + d2[1:])
    return s2 * LIFT_SCALE, d2[1:] / LIFT_SCALE


def low_rank(coupling, rank):
    rest, us, vs = coupling.copy(), [], []
    for _ in range(rank):
        i, j = np.unravel_index(np.argmax(np.abs(rest)), rest.shape)
        u, v = rest[:, j] / rest[i, j], rest[i, :].copy()
        us.append(u)
        vs.append(v)
        rest = rest - u[:, None] * v[None, :]
    assert np.abs(rest).max() < 1e-12
    return np.stack(us, 1), np.stack(vs, 0)


def block_maps(b):
    blocks = 5
    low, high = lift_matrix(blocks * b)
    low2, high2 = lift_matrix(blocks * b // 2)
    pairs = ((low, high, 2), (low2 @ low, high2 @ low, 4))
    levels = []
    for lows, highs, rank in pairs:
        n = lows.shape[0] // blocks

        def part(row, col):
            cols = slice(col * b, (col + 1) * b)
            rows = slice(row * n, (row + 1) * n)
            return np.concatenate([lows[rows, cols], highs[rows, cols]])

        for row in range(blocks):
            for col in range(blocks):
                if abs(row - col) > 1:
                    assert np.abs(part(row, col)).max() == 0
                elif row != col:
                    like = part(2, 2 + col - row)
                    assert np.abs(part(row, col) - like).max() < 1e-12
        assert np.abs(part(1, 1) - part(2, 2)).max() < 1e-12
        assert np.abs(part(3, 3) - part(2, 2)).max() < 1e-12
        own = [part(0, 0), part(2, 2), part(4, 4)]
        u_up, v_up = low_rank(part(2, 1), rank)
        u_down, v_down = low_rank(part(2, 3), rank)
        levels.append((own, {1: u_up, -1: u_down}, {1: v_up, -1: v_down}))
    return levels


@functools.lru_cache(maxsize=None)
def tables(bx, by, nz):
    low, high = lift_matrix(nz)
    low2, high2 = lift_matrix(nz // 2)
    depth1 = np.concatenate([low, high]).T
    depth2 = np.concatenate([low2, high2]).T
    levels_x, levels_y = block_maps(bx), block_maps(by)
    own_x, ux, vx = levels_x[1]
    own_y, uy, vy = levels_y[1]
    nx, ny = own_x[0].shape[0], own_y[0].shape[0]
    plane = []
    for cx in range(3):
        for cy in range(3):
            out = []
            for dx, dy in WAYS:
                m = np.kron(vx[dx] if dx else own_x[cx], vy[dy] if dy else own_y[cy])
                if dx == 0:
                    m = m.reshape(nx, -1, bx * by).transpose(1, 0, 2).reshape(-1, bx * by)
                out.append(m)
            out.append(np.kron(own_x[cx], own_y[cy]))
            plane.append(np.concatenate(out))
    columns = np.concatenate([u[d].T.reshape(-1) for u in (levels_y[0][1], uy) for d in (1, -1)])
    columns = np.repeat(columns[:, None], 128, axis=1)
    arrays = [t.astype(np.float32) for t in (depth1, depth2, np.stack(plane), columns)]
    return arrays, levels_x, levels_y


def dot(a, b):
    return jnp.dot(a, b, precision=HIGHEST, preferred_element_type=jnp.float32)


def lift_ends(e, o, prev, after, first, last):
    at, sub = jnp.where, lambda f, *lists: [f(*v) for v in zip(*lists)]
    e_after = after(e, sub(lambda p: at(last, p, 0.0), e))
    d1 = sub(lambda p, q, r: p + LIFT_ALPHA * (q + r), o, e, e_after)
    out1 = sub(lambda p: LIFT_ALPHA * p, e)
    d1_prev = prev(d1, sub(lambda p, q: at(first, p, q), d1, out1))
    s1 = sub(lambda p, q, r: p + LIFT_BETA * (q + r), e, d1_prev, d1)
    s1_after = after(s1, sub(lambda p, q: at(last, p, LIFT_BETA * q), s1, d1))
    d2 = sub(lambda p, q, r: p + LIFT_GAMMA * (q + r), d1, s1, s1_after)
    out2 = sub(lambda p, q: p + LIFT_GAMMA * (LIFT_BETA * p + q), out1, s1)
    d2_prev = prev(d2, sub(lambda p, q: at(first, p, q), d2, out2))
    s2 = sub(lambda p, q, r: p + LIFT_DELTA * (q + r), s1, d2_prev, d2)
    return [v * LIFT_SCALE for v in s2], [v * (1.0 / LIFT_SCALE) for v in d2]


def weighted(weights, values):
    terms = [float(w) * v for w, v in zip(weights, values) if w != 0.0]
    return functools.reduce(lambda p, q: p + q, terms)


def kernel(
    nx, ny, levels_x, levels_y, x_hbm, t1_hbm, t2_hbm, s2_hbm, uy_hbm, approx, two, one,
    x_v, t1_v, t2_v, s2_v, uy_v, xb, own1,
    face1_out, face1_in, corner1_out, corner1_in, out2, in2,
    load_sem, send1, recv1, send2, recv2,
):
    px, py = lax.axis_index("slab"), lax.axis_index("morton")
    not_first_x, last_x = lax.div(px + (nx - 2), nx - 1), lax.div(px, nx - 1)
    not_first_y, last_y = lax.div(py + (ny - 2), ny - 1), lax.div(py, ny - 1)
    here = (not_first_x + last_x) * 3 + not_first_y + last_y
    has_x = {1: 1 - last_x, -1: not_first_x, 0: 1}
    has_y = {1: 1 - last_y, -1: not_first_y, 0: 1}

    def exists(dx, dy):
        return has_x[dx] * has_y[dy] == 1

    def rows(ref, start, size):
        return ref.at[pl.ds(start, size)]

    loads = [
        pltpu.make_async_copy(source, target, load_sem.at[k])
        for k, (source, target) in enumerate((
            (x_hbm, x_v),
            (t1_hbm, t1_v),
            (t2_hbm, t2_v),
            (s2_hbm.at[here], s2_v),
            (uy_hbm, uy_v),
        ))
    ]
    for load in loads:
        load.start()

    barrier = pltpu.get_barrier_semaphore()
    for dx, dy in WAYS:
        @pl.when(exists(dx, dy))
        def _():
            pl.semaphore_signal(
                barrier, inc=1, device_id=(py + dy, px + dx), device_id_type=MESH
            )

    def message(level, k):
        dx, dy = WAYS[k]
        if level == 1 and k < 4:
            pair = rows(face1_out, k * 32, 32), rows(face1_in, k * 32, 32)
        elif level == 1:
            pair = corner1_out.at[k - 4], corner1_in.at[k - 4]
        elif k < 4:
            pair = rows(out2, k * 32, 32), rows(in2, k * 32, 32)
        else:
            pair = rows(out2, 64 + k * 16, 16), rows(in2, 64 + k * 16, 16)
        send, recv = (send1, recv1) if level == 1 else (send2, recv2)
        return pltpu.make_async_remote_copy(
            src_ref=pair[0],
            dst_ref=pair[1],
            send_sem=send.at[k],
            recv_sem=recv.at[k],
            device_id=(py + dy, px + dx),
            device_id_type=MESH,
        )

    def start(level):
        for k in ORDER:
            @pl.when(exists(*WAYS[k]))
            def _():
                message(level, k).start()

    def receive(level):
        for k in ORDER:
            dx, dy = WAYS[k]

            @pl.when(exists(-dx, -dy))
            def _():
                message(level, k).wait_recv()

    for k, (dx, dy) in enumerate(WAYS):
        @pl.when(jnp.logical_not(exists(-dx, -dy)))
        def _():
            if k < 4:
                face1_in[k * 32:k * 32 + 32, :] = jnp.zeros((32, 256), jnp.float32)
                in2[k * 32:k * 32 + 32, :] = jnp.zeros((32, 128), jnp.float32)
            else:
                corner1_in[k - 4] = jnp.zeros((4, 256), jnp.float32)
                in2[64 + k * 16:80 + k * 16, :] = jnp.zeros((16, 128), jnp.float32)

    loads[0].wait()
    loads[1].wait()
    z1 = dot(x_v[...].reshape(256, 256), t1_v[...])

    planes = [z1[16 * i:16 * i + 16, :] for i in range(16)]
    low, high = lift_ends(
        planes[0::2], planes[1::2],
        lambda v, end: [end[0]] + v[:-1],
        lambda v, end: v[1:] + [end[-1]],
        not_first_x == 0, last_x == 1,
    )
    _, ux, vx = levels_x[0]
    _, uy, vy = levels_y[0]
    along = [weighted(w, planes) for d in (1, -1) for w in vx[d]]
    for r, v in enumerate(low + high + along):
        for h in range(2):
            xb[320 * h + 16 * r:320 * h + 16 * r + 16, :] = v[:, 128 * h:128 * h + 128]

    def strided(begin, size, stride):
        return jnp.concatenate(
            [xb[pl.ds(320 * h + begin, size, stride=stride), :] for h in range(2)], axis=1
        )

    for kd, d in enumerate((1, -1)):
        for ky in range(2):
            taps = [y for y in range(16) if vy[d][ky, y] != 0.0]
            weights = [vy[d][ky, y] for y in taps]
            at = (2 + kd) * 32 + ky * 16
            face1_out[at:at + 16, :] = weighted(
                weights, [strided(y, 16, 16) for y in taps]
            )
            part = weighted(weights, [strided(256 + y, 4, 16) for y in taps])
            corner1_out[kd, 2 * ky:2 * ky + 2, :] = part[0:2]
            corner1_out[2 + kd, 2 * ky:2 * ky + 2, :] = part[2:4]

    place = lax.broadcasted_iota(jnp.int32, (8, 256), 0)
    for r in (16, 17, 18, 19) + tuple(range(16)):
        low, high = lift_ends(
            [strided(16 * r, 8, 2)], [strided(16 * r + 1, 8, 2)],
            lambda v, end: [jnp.where(place == 0, end[0], pltpu.roll(v[0], 1, 0))],
            lambda v, end: [jnp.where(place == 7, end[0], pltpu.roll(v[0], 7, 0))],
            not_first_y == 0, last_y == 1,
        )
        if r >= 16:
            at = (r - 16) * 16
            face1_out[at:at + 8, :] = low[0]
            face1_out[at + 8:at + 16, :] = high[0]
        else:
            own1[r, 0] = low[0]
            own1[r, 1] = high[0]
        if r == 19:
            pl.semaphore_wait(
                barrier,
                (1 + has_x[1] + has_x[-1]) * (1 + has_y[1] + has_y[-1]) - 1,
            )
            start(1)

    loads[2].wait()
    z2 = dot(z1[:, :128], t2_v[...])
    loads[3].wait()
    p2 = dot(s2_v[...], z2)
    out2[...] = p2[:192, :]
    start(2)
    own2 = p2[192:, :]
    loads[4].wait()

    receive(1)
    for bz in range(2):
        half = slice(bz * 128, bz * 128 + 128)
        column = [[[
            uy_v[((kd * 2 + ky) * 2 + b) * 8:((kd * 2 + ky) * 2 + b) * 8 + 8, :]
            for b in range(2)] for ky in range(2)] for kd in range(2)]

        def add_y(value, row, b):
            for kd in range(2):
                for ky in range(2):
                    value = value + row(kd, ky) * column[kd][ky][b]
            return value

        for b in range(2):
            side = [
                [
                    add_y(
                        face1_in[dx * 32 + kx * 16 + b * 8:dx * 32 + kx * 16 + b * 8 + 8, half],
                        lambda kd, ky: corner1_in[dx * 2 + kd, 2 * ky + kx:2 * ky + kx + 1, half],
                        b,
                    )
                    for kx in range(2)
                ]
                for dx in range(2)
            ]
            for r in range(16):
                band, i = 2 * (r // 8) + b, r % 8
                if band + bz == 0:
                    continue
                value = add_y(
                    own1[r, b, :, half],
                    lambda kd, ky: face1_in[
                        (2 + kd) * 32 + ky * 16 + r:(2 + kd) * 32 + ky * 16 + r + 1, half
                    ],
                    b,
                )
                for dx, d in enumerate((1, -1)):
                    if np.any(ux[d][r] != 0.0):
                        value = value + weighted(ux[d][r], side[dx])
                one[2 * band + bz - 1, i] = value

    receive(2)
    _, ux2, _ = levels_x[1]
    column2 = [uy_v[64 + k * 8:72 + k * 8, :] for k in range(8)]
    side2 = [
        [
            in2[dx * 32 + kx * 8:dx * 32 + kx * 8 + 8, :]
            + sum(
                in2[at:at + 1, :] * column2[kd * 4 + ky]
                for kd in range(2)
                for ky in range(4)
                for at in (128 + (dx * 2 + kd) * 16 + kx * 4 + ky,)
            )
            for kx in range(4)
        ]
        for dx in range(2)
    ]
    for r in range(8):
        value = own2[r * 8:r * 8 + 8, :] + sum(
            in2[at:at + 1, :] * column2[kd * 4 + ky]
            for kd in range(2)
            for ky in range(4)
            for at in ((2 + kd) * 32 + ky * 8 + r,)
        )
        for dx, d in enumerate((1, -1)):
            if np.any(ux2[d][r] != 0.0):
                value = value + weighted(ux2[d][r], side2[dx])
        for b in range(2):
            for bz in range(2):
                at, part = 4 * (r // 4) + 2 * b + bz, value[4 * b:4 * b + 4, 64 * bz:64 * bz + 64]
                if at:
                    two[at - 1, r % 4] = part
                else:
                    approx[r % 4] = part

    for level in (1, 2):
        for k in ORDER:
            @pl.when(exists(*WAYS[k]))
            def _():
                message(level, k).wait_send()


def store(approx_v, two_v, one_v, approx, two, one, sem):
    pairs = ((one_v, one), (two_v, two), (approx_v, approx))
    copies = [pltpu.make_async_copy(a, b, sem.at[k]) for k, (a, b) in enumerate(pairs)]
    for copy in copies:
        copy.start()
    for copy in copies:
        copy.wait()


def per_device(nx, ny, velocity):
    bx, by, nz = velocity.shape
    consts, levels_x, levels_y = tables(bx, by, nz)
    f32 = jnp.float32
    vmem = pl.BlockSpec(memory_space=pltpu.VMEM)
    held = [pltpu.VMEM(c.shape[-2:], f32) for c in consts]
    shapes = (
        (bx // 4, by // 4, nz // 4),
        (7, bx // 4, by // 4, nz // 4),
        (7, bx // 2, by // 2, nz // 2),
    )
    results = pl.pallas_call(
        functools.partial(kernel, nx, ny, levels_x, levels_y),
        out_shape=tuple(pltpu.VMEM(shape, f32) for shape in shapes),
        in_specs=[pl.BlockSpec(memory_space=pl.ANY)] * 5,
        out_specs=(vmem, vmem, vmem),
        scratch_shapes=[pltpu.VMEM((bx, by, nz), f32)]
        + held
        + [
            pltpu.VMEM((640, 128), f32),
            pltpu.VMEM((16, 2, 8, 256), f32),
            pltpu.VMEM((128, 256), f32),
            pltpu.VMEM((128, 256), f32),
            pltpu.VMEM((4, 4, 256), f32),
            pltpu.VMEM((4, 4, 256), f32),
            pltpu.VMEM((192, 128), f32),
            pltpu.VMEM((192, 128), f32),
            pltpu.SemaphoreType.DMA((5,)),
        ]
        + [pltpu.SemaphoreType.DMA((8,))] * 4,
        compiler_params=pltpu.CompilerParams(
            collective_id=0, has_side_effects=True, vmem_limit_bytes=60 * 1024 * 1024
        ),
    )(velocity, *[jnp.asarray(c) for c in consts])
    results = [pltpu.with_memory_space_constraint(r, pltpu.VMEM) for r in results]
    return pl.pallas_call(
        store,
        out_shape=tuple(jax.ShapeDtypeStruct(shape, f32) for shape in shapes),
        in_specs=[vmem] * 3,
        out_specs=[pl.BlockSpec(memory_space=pl.ANY)] * 3,
        scratch_shapes=[pltpu.SemaphoreType.DMA((3,))],
    )(*results)


def solution(mesh):
    placed = (P("slab", "morton", None),)
    return jax.shard_map(
        functools.partial(per_device, mesh.shape["slab"], mesh.shape["morton"]),
        mesh=mesh,
        in_specs=placed,
        out_specs=(
            P("slab", "morton", None),
            P(None, "slab", "morton", None),
            P(None, "slab", "morton", None),
        ),
        check_vma=False,
    )
```

```python
import functools

import jax
import jax.numpy as jnp
import numpy as np
from jax import lax
from jax.experimental import pallas as pl
from jax.experimental.pallas import tpu as pltpu
from jax.sharding import PartitionSpec as P

LIFT_ALPHA = -1.586134342059924
LIFT_BETA = -0.052980118572961
LIFT_GAMMA = 0.882911075530934
LIFT_DELTA = 0.443506852043971
LIFT_SCALE = 1.149604398860241

MESH = pl.DeviceIdType.MESH
FACES = ((1, 0), (-1, 0), (0, 1), (0, -1))
CORNERS = ((1, 1), (1, -1), (-1, 1), (-1, -1))
WAYS = FACES + CORNERS
ORDER = (7, 3, 5, 1, 0, 4, 6, 2)
HIGHEST = lax.Precision.HIGHEST


def lift_matrix(n):
    x = np.pad(np.eye(n), ((4, 4), (0, 0)), mode="reflect")
    e, o = x[0::2], x[1::2]
    d1 = o[:-1] + LIFT_ALPHA * (e[:-1] + e[1:])
    s1 = e[1:-1] + LIFT_BETA * (d1[:-1] + d1[1:])
    d2 = d1[1:-1] + LIFT_GAMMA * (s1[:-1] + s1[1:])
    s2 = s1[1:-1] + LIFT_DELTA * (d2[:-1] + d2[1:])
    return s2 * LIFT_SCALE, d2[1:] / LIFT_SCALE


def low_rank(coupling, rank):
    rest, us, vs = coupling.copy(), [], []
    for _ in range(rank):
        i, j = np.unravel_index(np.argmax(np.abs(rest)), rest.shape)
        u, v = rest[:, j] / rest[i, j], rest[i, :].copy()
        us.append(u)
        vs.append(v)
        rest = rest - u[:, None] * v[None, :]
    assert np.abs(rest).max() < 1e-12
    return np.stack(us, 1), np.stack(vs, 0)


def block_maps(b):
    blocks = 5
    low, high = lift_matrix(blocks * b)
    low2, high2 = lift_matrix(blocks * b // 2)
    pairs = ((low, high, 2), (low2 @ low, high2 @ low, 4))
    levels = []
    for lows, highs, rank in pairs:
        n = lows.shape[0] // blocks

        def part(row, col):
            cols = slice(col * b, (col + 1) * b)
            rows = slice(row * n, (row + 1) * n)
            return np.concatenate([lows[rows, cols], highs[rows, cols]])

        for row in range(blocks):
            for col in range(blocks):
                if abs(row - col) > 1:
                    assert np.abs(part(row, col)).max() == 0
                elif row != col:
                    like = part(2, 2 + col - row)
                    assert np.abs(part(row, col) - like).max() < 1e-12
        assert np.abs(part(1, 1) - part(2, 2)).max() < 1e-12
        assert np.abs(part(3, 3) - part(2, 2)).max() < 1e-12
        own = [part(0, 0), part(2, 2), part(4, 4)]
        u_up, v_up = low_rank(part(2, 1), rank)
        u_down, v_down = low_rank(part(2, 3), rank)
        levels.append((own, {1: u_up, -1: u_down}, {1: v_up, -1: v_down}))
    return levels


@functools.lru_cache(maxsize=None)
def tables(bx, by, nz):
    low, high = lift_matrix(nz)
    low2, high2 = lift_matrix(nz // 2)
    depth1 = np.concatenate([low, high]).T
    depth2 = np.concatenate([low2, high2]).T
    levels_x, levels_y = block_maps(bx), block_maps(by)
    own_x, ux, vx = levels_x[1]
    own_y, uy, vy = levels_y[1]
    nx, ny = own_x[0].shape[0], own_y[0].shape[0]
    plane = []
    for cx in range(3):
        for cy in range(3):
            out = []
            for dx, dy in WAYS:
                m = np.kron(vx[dx] if dx else own_x[cx], vy[dy] if dy else own_y[cy])
                if dx == 0:
                    m = m.reshape(nx, -1, bx * by).transpose(1, 0, 2).reshape(-1, bx * by)
                out.append(m)
            out.append(np.kron(own_x[cx], own_y[cy]))
            plane.append(np.concatenate(out))
    columns = np.concatenate([u[d].T.reshape(-1) for u in (levels_y[0][1], uy) for d in (1, -1)])
    columns = np.repeat(columns[:, None], 128, axis=1)
    arrays = [t.astype(np.float32) for t in (depth1, depth2, np.stack(plane), columns)]
    return arrays, levels_x, levels_y


def dot(a, b):
    return jnp.dot(a, b, precision=HIGHEST, preferred_element_type=jnp.float32)


def lift_ends(e, o, prev, after, first, last):
    at, sub = jnp.where, lambda f, *lists: [f(*v) for v in zip(*lists)]
    e_after = after(e, sub(lambda p: at(last, p, 0.0), e))
    d1 = sub(lambda p, q, r: p + LIFT_ALPHA * (q + r), o, e, e_after)
    out1 = sub(lambda p: LIFT_ALPHA * p, e)
    d1_prev = prev(d1, sub(lambda p, q: at(first, p, q), d1, out1))
    s1 = sub(lambda p, q, r: p + LIFT_BETA * (q + r), e, d1_prev, d1)
    s1_after = after(s1, sub(lambda p, q: at(last, p, LIFT_BETA * q), s1, d1))
    d2 = sub(lambda p, q, r: p + LIFT_GAMMA * (q + r), d1, s1, s1_after)
    out2 = sub(lambda p, q: p + LIFT_GAMMA * (LIFT_BETA * p + q), out1, s1)
    d2_prev = prev(d2, sub(lambda p, q: at(first, p, q), d2, out2))
    s2 = sub(lambda p, q, r: p + LIFT_DELTA * (q + r), s1, d2_prev, d2)
    return [v * LIFT_SCALE for v in s2], [v * (1.0 / LIFT_SCALE) for v in d2]


def weighted(weights, values):
    terms = [float(w) * v for w, v in zip(weights, values) if w != 0.0]
    return functools.reduce(lambda p, q: p + q, terms)


def kernel(
    nx, ny, levels_x, levels_y, x_hbm, t1_hbm, t2_hbm, s2_hbm, uy_hbm, approx, two, one,
    x_v, t1_v, t2_v, s2_v, uy_v, xb, own1,
    face1_out, face1_in, corner1_out, corner1_in, out2, in2,
    load_sem, send1, recv1, send2, recv2,
):
    px, py = lax.axis_index("slab"), lax.axis_index("morton")
    has_x = {1: jnp.minimum(nx - 1 - px, 1), -1: jnp.minimum(px, 1), 0: 1}
    has_y = {1: jnp.minimum(ny - 1 - py, 1), -1: jnp.minimum(py, 1), 0: 1}
    here = (has_x[-1] - has_x[1] + 1) * 3 + has_y[-1] - has_y[1] + 1

    def exists(dx, dy):
        return has_x[dx] * has_y[dy] == 1

    def rows(ref, start, size):
        return ref.at[pl.ds(start, size)]

    loads = [
        pltpu.make_async_copy(source, target, load_sem.at[k])
        for k, (source, target) in enumerate((
            (rows(x_hbm, 0, 8), rows(x_v, 0, 8)),
            (rows(t1_hbm, 0, 128), rows(t1_v, 0, 128)),
            (rows(x_hbm, 8, 8), rows(x_v, 8, 8)),
            (rows(t1_hbm, 128, 128), rows(t1_v, 128, 128)),
            (t2_hbm, t2_v),
            (s2_hbm.at[here], s2_v),
            (uy_hbm, uy_v),
        ))
    ]
    for load in loads:
        load.start()

    barrier = pltpu.get_barrier_semaphore()
    for dx, dy in WAYS:
        @pl.when(exists(dx, dy))
        def _():
            pl.semaphore_signal(
                barrier, inc=1, device_id=(py + dy, px + dx), device_id_type=MESH
            )

    def message(level, k):
        dx, dy = WAYS[k]
        if level == 1 and k < 4:
            pair = rows(face1_out, k * 32, 32), rows(face1_in, k * 32, 32)
        elif level == 1:
            pair = corner1_out.at[k - 4], corner1_in.at[k - 4]
        elif k < 4:
            pair = rows(out2, k * 32, 32), rows(in2, k * 32, 32)
        else:
            pair = rows(out2, 64 + k * 16, 16), rows(in2, 64 + k * 16, 16)
        send, recv = (send1, recv1) if level == 1 else (send2, recv2)
        return pltpu.make_async_remote_copy(
            src_ref=pair[0],
            dst_ref=pair[1],
            send_sem=send.at[k],
            recv_sem=recv.at[k],
            device_id=(py + dy, px + dx),
            device_id_type=MESH,
        )

    def start(level):
        for k in ORDER:
            @pl.when(exists(*WAYS[k]))
            def _():
                message(level, k).start()

    def receive(level):
        for k in ORDER:
            dx, dy = WAYS[k]

            @pl.when(exists(-dx, -dy))
            def _():
                message(level, k).wait_recv()

    for k, (dx, dy) in enumerate(WAYS):
        @pl.when(jnp.logical_not(exists(-dx, -dy)))
        def _():
            if k < 4:
                face1_in[k * 32:k * 32 + 32, :] = jnp.zeros((32, 256), jnp.float32)
                in2[k * 32:k * 32 + 32, :] = jnp.zeros((32, 128), jnp.float32)
            else:
                corner1_in[k - 4] = jnp.zeros((4, 256), jnp.float32)
                in2[64 + k * 16:80 + k * 16, :] = jnp.zeros((16, 128), jnp.float32)

    for load in loads[:4]:
        load.wait()
    z1 = dot(x_v[...].reshape(256, 256), t1_v[...])

    planes = [z1[16 * i:16 * i + 16, :] for i in range(16)]
    low, high = lift_ends(
        planes[0::2], planes[1::2],
        lambda v, end: [end[0]] + v[:-1],
        lambda v, end: v[1:] + [end[-1]],
        px == 0, px == nx - 1,
    )
    _, ux, vx = levels_x[0]
    _, uy, vy = levels_y[0]
    along = [weighted(w, planes) for d in (1, -1) for w in vx[d]]
    for r, v in enumerate(low + high + along):
        for h in range(2):
            xb[320 * h + 16 * r:320 * h + 16 * r + 16, :] = v[:, 128 * h:128 * h + 128]

    def strided(begin, size, stride):
        return jnp.concatenate(
            [xb[pl.ds(320 * h + begin, size, stride=stride), :] for h in range(2)], axis=1
        )

    for kd, d in enumerate((1, -1)):
        for ky in range(2):
            taps = [y for y in range(16) if vy[d][ky, y] != 0.0]
            weights = [vy[d][ky, y] for y in taps]
            at = (2 + kd) * 32 + ky * 16
            face1_out[at:at + 16, :] = weighted(
                weights, [strided(y, 16, 16) for y in taps]
            )
            part = weighted(weights, [strided(256 + y, 4, 16) for y in taps])
            corner1_out[kd, 2 * ky:2 * ky + 2, :] = part[0:2]
            corner1_out[2 + kd, 2 * ky:2 * ky + 2, :] = part[2:4]

    place = lax.broadcasted_iota(jnp.int32, (8, 256), 0)
    for r in (16, 17, 18, 19) + tuple(range(16)):
        low, high = lift_ends(
            [strided(16 * r, 8, 2)], [strided(16 * r + 1, 8, 2)],
            lambda v, end: [jnp.where(place == 0, end[0], pltpu.roll(v[0], 1, 0))],
            lambda v, end: [jnp.where(place == 7, end[0], pltpu.roll(v[0], 7, 0))],
            py == 0, py == ny - 1,
        )
        if r >= 16:
            at = (r - 16) * 16
            face1_out[at:at + 8, :] = low[0]
            face1_out[at + 8:at + 16, :] = high[0]
        else:
            own1[r, 0] = low[0]
            own1[r, 1] = high[0]
        if r == 19:
            pl.semaphore_wait(
                barrier,
                (1 + has_x[1] + has_x[-1]) * (1 + has_y[1] + has_y[-1]) - 1,
            )
            start(1)

    loads[4].wait()
    z2 = dot(z1[:, :128], t2_v[...])
    loads[5].wait()
    p2 = dot(s2_v[...], z2)
    out2[...] = p2[:192, :]
    start(2)
    own2 = p2[192:, :]
    loads[6].wait()

    receive(1)
    for bz in range(2):
        half = slice(bz * 128, bz * 128 + 128)
        column = [[[
            uy_v[((kd * 2 + ky) * 2 + b) * 8:((kd * 2 + ky) * 2 + b) * 8 + 8, :]
            for b in range(2)] for ky in range(2)] for kd in range(2)]

        def add_y(value, row, b):
            for kd in range(2):
                for ky in range(2):
                    value = value + row(kd, ky) * column[kd][ky][b]
            return value

        for b in range(2):
            side = [
                [
                    add_y(
                        face1_in[dx * 32 + kx * 16 + b * 8:dx * 32 + kx * 16 + b * 8 + 8, half],
                        lambda kd, ky: corner1_in[dx * 2 + kd, 2 * ky + kx:2 * ky + kx + 1, half],
                        b,
                    )
                    for kx in range(2)
                ]
                for dx in range(2)
            ]
            for r in range(16):
                band, i = 2 * (r // 8) + b, r % 8
                if band + bz == 0:
                    continue
                value = add_y(
                    own1[r, b, :, half],
                    lambda kd, ky: face1_in[
                        (2 + kd) * 32 + ky * 16 + r:(2 + kd) * 32 + ky * 16 + r + 1, half
                    ],
                    b,
                )
                for dx, d in enumerate((1, -1)):
                    if np.any(ux[d][r] != 0.0):
                        value = value + weighted(ux[d][r], side[dx])
                one[2 * band + bz - 1, i] = value

    for level in (1, 2):
        for k in ORDER:
            @pl.when(exists(*WAYS[k]))
            def _():
                message(level, k).wait_send()

    receive(2)
    _, ux2, _ = levels_x[1]
    column2 = [uy_v[64 + k * 8:72 + k * 8, :] for k in range(8)]
    side2 = [
        [
            in2[dx * 32 + kx * 8:dx * 32 + kx * 8 + 8, :]
            + sum(
                in2[at:at + 1, :] * column2[kd * 4 + ky]
                for kd in range(2)
                for ky in range(4)
                for at in (128 + (dx * 2 + kd) * 16 + kx * 4 + ky,)
            )
            for kx in range(4)
        ]
        for dx in range(2)
    ]
    for r in range(8):
        value = own2[r * 8:r * 8 + 8, :] + sum(
            in2[at:at + 1, :] * column2[kd * 4 + ky]
            for kd in range(2)
            for ky in range(4)
            for at in ((2 + kd) * 32 + ky * 8 + r,)
        )
        for dx, d in enumerate((1, -1)):
            if np.any(ux2[d][r] != 0.0):
                value = value + weighted(ux2[d][r], side2[dx])
        for b in range(2):
            for bz in range(2):
                at, part = 4 * (r // 4) + 2 * b + bz, value[4 * b:4 * b + 4, 64 * bz:64 * bz + 64]
                if at:
                    two[at - 1, r % 4] = part
                else:
                    approx[r % 4] = part


def store(approx_v, two_v, one_v, approx, two, one, sem):
    pairs = ((one_v, one), (two_v, two), (approx_v, approx))
    copies = [pltpu.make_async_copy(a, b, sem.at[k]) for k, (a, b) in enumerate(pairs)]
    for copy in copies:
        copy.start()
    for copy in copies:
        copy.wait()


def per_device(nx, ny, velocity):
    bx, by, nz = velocity.shape
    consts, levels_x, levels_y = tables(bx, by, nz)
    f32 = jnp.float32
    vmem = pl.BlockSpec(memory_space=pltpu.VMEM)
    held = [pltpu.VMEM(c.shape[-2:], f32) for c in consts]
    shapes = (
        (bx // 4, by // 4, nz // 4),
        (7, bx // 4, by // 4, nz // 4),
        (7, bx // 2, by // 2, nz // 2),
    )
    results = pl.pallas_call(
        functools.partial(kernel, nx, ny, levels_x, levels_y),
        out_shape=tuple(pltpu.VMEM(shape, f32) for shape in shapes),
        in_specs=[pl.BlockSpec(memory_space=pl.ANY)] * 5,
        out_specs=(vmem, vmem, vmem),
        scratch_shapes=[pltpu.VMEM((bx, by, nz), f32)]
        + held
        + [
            pltpu.VMEM((640, 128), f32),
            pltpu.VMEM((16, 2, 8, 256), f32),
            pltpu.VMEM((128, 256), f32),
            pltpu.VMEM((128, 256), f32),
            pltpu.VMEM((4, 4, 256), f32),
            pltpu.VMEM((4, 4, 256), f32),
            pltpu.VMEM((192, 128), f32),
            pltpu.VMEM((192, 128), f32),
            pltpu.SemaphoreType.DMA((7,)),
        ]
        + [pltpu.SemaphoreType.DMA((8,))] * 4,
        compiler_params=pltpu.CompilerParams(
            collective_id=0, has_side_effects=True, vmem_limit_bytes=60 * 1024 * 1024
        ),
    )(velocity, *[jnp.asarray(c) for c in consts])
    results = [pltpu.with_memory_space_constraint(r, pltpu.VMEM) for r in results]
    return pl.pallas_call(
        store,
        out_shape=tuple(jax.ShapeDtypeStruct(shape, f32) for shape in shapes),
        in_specs=[vmem] * 3,
        out_specs=[pl.BlockSpec(memory_space=pl.ANY)] * 3,
        scratch_shapes=[pltpu.SemaphoreType.DMA((3,))],
    )(*results)


def solution(mesh):
    placed = (P("slab", "morton", None),)
    return jax.shard_map(
        functools.partial(per_device, mesh.shape["slab"], mesh.shape["morton"]),
        mesh=mesh,
        in_specs=placed,
        out_specs=(
            P("slab", "morton", None),
            P(None, "slab", "morton", None),
            P(None, "slab", "morton", None),
        ),
        check_vma=False,
    )
```

```python
import functools

import jax
import jax.numpy as jnp
import numpy as np
from jax import lax
from jax.experimental import pallas as pl
from jax.experimental.pallas import tpu as pltpu
from jax.sharding import PartitionSpec as P

LIFT_ALPHA = -1.586134342059924
LIFT_BETA = -0.052980118572961
LIFT_GAMMA = 0.882911075530934
LIFT_DELTA = 0.443506852043971
LIFT_SCALE = 1.149604398860241

MESH = pl.DeviceIdType.MESH
FACES = ((1, 0), (-1, 0), (0, 1), (0, -1))
CORNERS = ((1, 1), (1, -1), (-1, 1), (-1, -1))
WAYS = FACES + CORNERS
ORDER = (7, 3, 5, 1, 0, 4, 6, 2)
HIGHEST = lax.Precision.HIGHEST


def lift_matrix(n):
    x = np.pad(np.eye(n), ((4, 4), (0, 0)), mode="reflect")
    e, o = x[0::2], x[1::2]
    d1 = o[:-1] + LIFT_ALPHA * (e[:-1] + e[1:])
    s1 = e[1:-1] + LIFT_BETA * (d1[:-1] + d1[1:])
    d2 = d1[1:-1] + LIFT_GAMMA * (s1[:-1] + s1[1:])
    s2 = s1[1:-1] + LIFT_DELTA * (d2[:-1] + d2[1:])
    return s2 * LIFT_SCALE, d2[1:] / LIFT_SCALE


def low_rank(coupling, rank):
    rest, us, vs = coupling.copy(), [], []
    for _ in range(rank):
        i, j = np.unravel_index(np.argmax(np.abs(rest)), rest.shape)
        u, v = rest[:, j] / rest[i, j], rest[i, :].copy()
        us.append(u)
        vs.append(v)
        rest = rest - u[:, None] * v[None, :]
    assert np.abs(rest).max() < 1e-12
    return np.stack(us, 1), np.stack(vs, 0)


def block_maps(b):
    blocks = 5
    low, high = lift_matrix(blocks * b)
    low2, high2 = lift_matrix(blocks * b // 2)
    pairs = ((low, high, 2), (low2 @ low, high2 @ low, 4))
    levels = []
    for lows, highs, rank in pairs:
        n = lows.shape[0] // blocks

        def part(row, col):
            cols = slice(col * b, (col + 1) * b)
            rows = slice(row * n, (row + 1) * n)
            return np.concatenate([lows[rows, cols], highs[rows, cols]])

        for row in range(blocks):
            for col in range(blocks):
                if abs(row - col) > 1:
                    assert np.abs(part(row, col)).max() == 0
                elif row != col:
                    like = part(2, 2 + col - row)
                    assert np.abs(part(row, col) - like).max() < 1e-12
        assert np.abs(part(1, 1) - part(2, 2)).max() < 1e-12
        assert np.abs(part(3, 3) - part(2, 2)).max() < 1e-12
        own = [part(0, 0), part(2, 2), part(4, 4)]
        u_up, v_up = low_rank(part(2, 1), rank)
        u_down, v_down = low_rank(part(2, 3), rank)
        levels.append((own, {1: u_up, -1: u_down}, {1: v_up, -1: v_down}))
    return levels


@functools.lru_cache(maxsize=None)
def tables(bx, by, nz):
    low2, high2 = lift_matrix(nz // 2)
    depth2 = np.concatenate([low2, high2]).T
    levels_x, levels_y = block_maps(bx), block_maps(by)
    own_x, ux, vx = levels_x[1]
    own_y, uy, vy = levels_y[1]
    nx, ny = own_x[0].shape[0], own_y[0].shape[0]
    plane = []
    for cx in range(3):
        for cy in range(3):
            out = []
            for dx, dy in WAYS:
                m = np.kron(vx[dx] if dx else own_x[cx], vy[dy] if dy else own_y[cy])
                if dx == 0:
                    m = m.reshape(nx, -1, bx * by).transpose(1, 0, 2).reshape(-1, bx * by)
                out.append(m)
            out.append(np.kron(own_x[cx], own_y[cy]))
            plane.append(np.concatenate(out))
    columns = np.concatenate([u[d].T.reshape(-1) for u in (levels_y[0][1], uy) for d in (1, -1)])
    columns = np.repeat(columns[:, None], 128, axis=1)
    arrays = [t.astype(np.float32) for t in (depth2, np.stack(plane), columns)]
    return arrays, levels_x, levels_y


def dot(a, b):
    return jnp.dot(a, b, precision=HIGHEST, preferred_element_type=jnp.float32)


def lift_ends(e, o, prev, after, first, last):
    def at(grid_end, p, q):
        return p if grid_end is True else jnp.where(grid_end, p, q)

    sub = lambda f, *lists: [f(*v) for v in zip(*lists)]
    e_after = after(e, sub(lambda p: at(last, p, 0.0), e))
    d1 = sub(lambda p, q, r: p + LIFT_ALPHA * (q + r), o, e, e_after)
    out1 = sub(lambda p: LIFT_ALPHA * p, e)
    d1_prev = prev(d1, sub(lambda p, q: at(first, p, q), d1, out1))
    s1 = sub(lambda p, q, r: p + LIFT_BETA * (q + r), e, d1_prev, d1)
    s1_after = after(s1, sub(lambda p, q: at(last, p, LIFT_BETA * q), s1, d1))
    d2 = sub(lambda p, q, r: p + LIFT_GAMMA * (q + r), d1, s1, s1_after)
    out2 = sub(lambda p, q: p + LIFT_GAMMA * (LIFT_BETA * p + q), out1, s1)
    d2_prev = prev(d2, sub(lambda p, q: at(first, p, q), d2, out2))
    s2 = sub(lambda p, q, r: p + LIFT_DELTA * (q + r), s1, d2_prev, d2)
    return [v * LIFT_SCALE for v in s2], [v * (1.0 / LIFT_SCALE) for v in d2]


def weighted(weights, values):
    terms = [float(w) * v for w, v in zip(weights, values) if w != 0.0]
    return functools.reduce(lambda p, q: p + q, terms)


def kernel(
    nx, ny, levels_x, levels_y, x_hbm, t2_hbm, s2_hbm, uy_hbm, approx, two, one,
    x_v, t2_v, s2_v, uy_v, xb, own1,
    face1_out, face1_in, corner1_out, corner1_in, out2, in2,
    load_sem, send1, recv1, send2, recv2,
):
    px, py = lax.axis_index("slab"), lax.axis_index("morton")
    has_x = {1: jnp.minimum(nx - 1 - px, 1), -1: jnp.minimum(px, 1), 0: 1}
    has_y = {1: jnp.minimum(ny - 1 - py, 1), -1: jnp.minimum(py, 1), 0: 1}
    here = (has_x[-1] - has_x[1] + 1) * 3 + has_y[-1] - has_y[1] + 1

    def exists(dx, dy):
        return has_x[dx] * has_y[dy] == 1

    def rows(ref, start, size):
        return ref.at[pl.ds(start, size)]

    loads = [
        pltpu.make_async_copy(source, target, load_sem.at[k])
        for k, (source, target) in enumerate((
            (rows(x_hbm, 0, 8), rows(x_v, 0, 8)),
            (rows(x_hbm, 8, 8), rows(x_v, 8, 8)),
            (t2_hbm, t2_v),
            (s2_hbm.at[here], s2_v),
            (uy_hbm, uy_v),
        ))
    ]
    for load in loads:
        load.start()

    barrier = pltpu.get_barrier_semaphore()
    for dx, dy in WAYS:
        @pl.when(exists(dx, dy))
        def _():
            pl.semaphore_signal(
                barrier, inc=1, device_id=(py + dy, px + dx), device_id_type=MESH
            )

    def message(level, k):
        dx, dy = WAYS[k]
        if level == 1 and k < 4:
            pair = rows(face1_out, k * 32, 32), rows(face1_in, k * 32, 32)
        elif level == 1:
            pair = corner1_out.at[k - 4], corner1_in.at[k - 4]
        elif k < 4:
            pair = rows(out2, k * 32, 32), rows(in2, k * 32, 32)
        else:
            pair = rows(out2, 64 + k * 16, 16), rows(in2, 64 + k * 16, 16)
        send, recv = (send1, recv1) if level == 1 else (send2, recv2)
        return pltpu.make_async_remote_copy(
            src_ref=pair[0],
            dst_ref=pair[1],
            send_sem=send.at[k],
            recv_sem=recv.at[k],
            device_id=(py + dy, px + dx),
            device_id_type=MESH,
        )

    def start(level):
        for k in ORDER:
            @pl.when(exists(*WAYS[k]))
            def _():
                message(level, k).start()

    def receive(level):
        for k in ORDER:
            dx, dy = WAYS[k]

            @pl.when(exists(-dx, -dy))
            def _():
                message(level, k).wait_recv()

    for k, (dx, dy) in enumerate(WAYS):
        @pl.when(jnp.logical_not(exists(-dx, -dy)))
        def _():
            if k < 4:
                face1_in[k * 32:k * 32 + 32, :] = jnp.zeros((32, 256), jnp.float32)
                in2[k * 32:k * 32 + 32, :] = jnp.zeros((32, 128), jnp.float32)
            else:
                corner1_in[k - 4] = jnp.zeros((4, 256), jnp.float32)
                in2[64 + k * 16:80 + k * 16, :] = jnp.zeros((16, 128), jnp.float32)

    lane = lax.broadcasted_iota(jnp.int32, (16, 128), 1)
    left = lane < 64
    cell = 2 * lane
    to_left = jnp.where(left, cell, cell - 127)
    to_right = jnp.where(left, cell + 1, cell - 128)
    planes = []
    for k in range(2):
        loads[k].wait()
        for i in range(8 * k, 8 * k + 8):
            p = jnp.take_along_axis(x_v[i, :, :128], to_left, axis=1)
            q = jnp.take_along_axis(x_v[i, :, 128:], to_right, axis=1)
            low, high = lift_ends(
                [jnp.where(left, p, q)], [pltpu.roll(jnp.where(left, q, p), 64, 1)],
                lambda v, end: [jnp.where(lane == 0, end[0], pltpu.roll(v[0], 1, 1))],
                lambda v, end: [jnp.where(lane == 127, end[0], pltpu.roll(v[0], 127, 1))],
                True, True,
            )
            planes.append(jnp.concatenate([low[0], high[0]], axis=1))
    loads[2].wait()
    z2 = dot(jnp.concatenate([p[:, :128] for p in planes], axis=0), t2_v[...])

    low, high = lift_ends(
        planes[0::2], planes[1::2],
        lambda v, end: [end[0]] + v[:-1],
        lambda v, end: v[1:] + [end[-1]],
        px == 0, px == nx - 1,
    )
    _, ux, vx = levels_x[0]
    _, uy, vy = levels_y[0]
    along = [weighted(w, planes) for d in (1, -1) for w in vx[d]]
    for r, v in enumerate(low + high + along):
        for h in range(2):
            xb[320 * h + 16 * r:320 * h + 16 * r + 16, :] = v[:, 128 * h:128 * h + 128]

    def strided(begin, size, stride):
        return jnp.concatenate(
            [xb[pl.ds(320 * h + begin, size, stride=stride), :] for h in range(2)], axis=1
        )

    for kd, d in enumerate((1, -1)):
        for ky in range(2):
            taps = [y for y in range(16) if vy[d][ky, y] != 0.0]
            weights = [vy[d][ky, y] for y in taps]
            at = (2 + kd) * 32 + ky * 16
            face1_out[at:at + 16, :] = weighted(
                weights, [strided(y, 16, 16) for y in taps]
            )
            part = weighted(weights, [strided(256 + y, 4, 16) for y in taps])
            corner1_out[kd, 2 * ky:2 * ky + 2, :] = part[0:2]
            corner1_out[2 + kd, 2 * ky:2 * ky + 2, :] = part[2:4]

    place = lax.broadcasted_iota(jnp.int32, (8, 256), 0)
    for r in (16, 17, 18, 19) + tuple(range(16)):
        low, high = lift_ends(
            [strided(16 * r, 8, 2)], [strided(16 * r + 1, 8, 2)],
            lambda v, end: [jnp.where(place == 0, end[0], pltpu.roll(v[0], 1, 0))],
            lambda v, end: [jnp.where(place == 7, end[0], pltpu.roll(v[0], 7, 0))],
            py == 0, py == ny - 1,
        )
        if r >= 16:
            at = (r - 16) * 16
            face1_out[at:at + 8, :] = low[0]
            face1_out[at + 8:at + 16, :] = high[0]
        else:
            own1[r, 0] = low[0]
            own1[r, 1] = high[0]
        if r == 19:
            pl.semaphore_wait(
                barrier,
                (1 + has_x[1] + has_x[-1]) * (1 + has_y[1] + has_y[-1]) - 1,
            )
            start(1)

    loads[3].wait()
    p2 = dot(s2_v[...], z2)
    out2[...] = p2[:192, :]
    start(2)
    own2 = p2[192:, :]
    loads[4].wait()

    receive(1)
    for bz in range(2):
        half = slice(bz * 128, bz * 128 + 128)
        column = [[[
            uy_v[((kd * 2 + ky) * 2 + b) * 8:((kd * 2 + ky) * 2 + b) * 8 + 8, :]
            for b in range(2)] for ky in range(2)] for kd in range(2)]

        def add_y(value, row, b):
            for kd in range(2):
                for ky in range(2):
                    value = value + row(kd, ky) * column[kd][ky][b]
            return value

        for b in range(2):
            side = [
                [
                    add_y(
                        face1_in[dx * 32 + kx * 16 + b * 8:dx * 32 + kx * 16 + b * 8 + 8, half],
                        lambda kd, ky: corner1_in[dx * 2 + kd, 2 * ky + kx:2 * ky + kx + 1, half],
                        b,
                    )
                    for kx in range(2)
                ]
                for dx in range(2)
            ]
            for r in range(16):
                band, i = 2 * (r // 8) + b, r % 8
                if band + bz == 0:
                    continue
                value = add_y(
                    own1[r, b, :, half],
                    lambda kd, ky: face1_in[
                        (2 + kd) * 32 + ky * 16 + r:(2 + kd) * 32 + ky * 16 + r + 1, half
                    ],
                    b,
                )
                for dx, d in enumerate((1, -1)):
                    if np.any(ux[d][r] != 0.0):
                        value = value + weighted(ux[d][r], side[dx])
                one[2 * band + bz - 1, i] = value

    for level in (1, 2):
        for k in ORDER:
            @pl.when(exists(*WAYS[k]))
            def _():
                message(level, k).wait_send()

    receive(2)
    _, ux2, _ = levels_x[1]
    column2 = [uy_v[64 + k * 8:72 + k * 8, :] for k in range(8)]
    side2 = [
        [
            in2[dx * 32 + kx * 8:dx * 32 + kx * 8 + 8, :]
            + sum(
                in2[at:at + 1, :] * column2[kd * 4 + ky]
                for kd in range(2)
                for ky in range(4)
                for at in (128 + (dx * 2 + kd) * 16 + kx * 4 + ky,)
            )
            for kx in range(4)
        ]
        for dx in range(2)
    ]
    for r in range(8):
        value = own2[r * 8:r * 8 + 8, :] + sum(
            in2[at:at + 1, :] * column2[kd * 4 + ky]
            for kd in range(2)
            for ky in range(4)
            for at in ((2 + kd) * 32 + ky * 8 + r,)
        )
        for dx, d in enumerate((1, -1)):
            if np.any(ux2[d][r] != 0.0):
                value = value + weighted(ux2[d][r], side2[dx])
        for b in range(2):
            for bz in range(2):
                at, part = 4 * (r // 4) + 2 * b + bz, value[4 * b:4 * b + 4, 64 * bz:64 * bz + 64]
                if at:
                    two[at - 1, r % 4] = part
                else:
                    approx[r % 4] = part


def store(approx_v, two_v, one_v, approx, two, one, sem):
    pairs = ((one_v, one), (two_v, two), (approx_v, approx))
    copies = [pltpu.make_async_copy(a, b, sem.at[k]) for k, (a, b) in enumerate(pairs)]
    for copy in copies:
        copy.start()
    for copy in copies:
        copy.wait()


def per_device(nx, ny, velocity):
    bx, by, nz = velocity.shape
    consts, levels_x, levels_y = tables(bx, by, nz)
    f32 = jnp.float32
    vmem = pl.BlockSpec(memory_space=pltpu.VMEM)
    held = [pltpu.VMEM(c.shape[-2:], f32) for c in consts]
    shapes = (
        (bx // 4, by // 4, nz // 4),
        (7, bx // 4, by // 4, nz // 4),
        (7, bx // 2, by // 2, nz // 2),
    )
    results = pl.pallas_call(
        functools.partial(kernel, nx, ny, levels_x, levels_y),
        out_shape=tuple(pltpu.VMEM(shape, f32) for shape in shapes),
        in_specs=[pl.BlockSpec(memory_space=pl.ANY)] * 4,
        out_specs=(vmem, vmem, vmem),
        scratch_shapes=[pltpu.VMEM((bx, by, nz), f32)]
        + held
        + [
            pltpu.VMEM((640, 128), f32),
            pltpu.VMEM((16, 2, 8, 256), f32),
            pltpu.VMEM((128, 256), f32),
            pltpu.VMEM((128, 256), f32),
            pltpu.VMEM((4, 4, 256), f32),
            pltpu.VMEM((4, 4, 256), f32),
            pltpu.VMEM((192, 128), f32),
            pltpu.VMEM((192, 128), f32),
            pltpu.SemaphoreType.DMA((5,)),
        ]
        + [pltpu.SemaphoreType.DMA((8,))] * 4,
        compiler_params=pltpu.CompilerParams(
            collective_id=0, has_side_effects=True, vmem_limit_bytes=60 * 1024 * 1024
        ),
    )(velocity, *[jnp.asarray(c) for c in consts])
    results = [pltpu.with_memory_space_constraint(r, pltpu.VMEM) for r in results]
    return pl.pallas_call(
        store,
        out_shape=tuple(jax.ShapeDtypeStruct(shape, f32) for shape in shapes),
        in_specs=[vmem] * 3,
        out_specs=[pl.BlockSpec(memory_space=pl.ANY)] * 3,
        scratch_shapes=[pltpu.SemaphoreType.DMA((3,))],
    )(*results)


def solution(mesh):
    placed = (P("slab", "morton", None),)
    return jax.shard_map(
        functools.partial(per_device, mesh.shape["slab"], mesh.shape["morton"]),
        mesh=mesh,
        in_specs=placed,
        out_specs=(
            P("slab", "morton", None),
            P(None, "slab", "morton", None),
            P(None, "slab", "morton", None),
        ),
        check_vma=False,
    )
```

```python
import functools

import jax
import jax.numpy as jnp
import numpy as np
from jax import lax
from jax.experimental import pallas as pl
from jax.experimental.pallas import tpu as pltpu
from jax.sharding import PartitionSpec as P

LIFT_ALPHA = -1.586134342059924
LIFT_BETA = -0.052980118572961
LIFT_GAMMA = 0.882911075530934
LIFT_DELTA = 0.443506852043971
LIFT_SCALE = 1.149604398860241

MESH = pl.DeviceIdType.MESH
FACES = ((1, 0), (-1, 0), (0, 1), (0, -1))
CORNERS = ((1, 1), (1, -1), (-1, 1), (-1, -1))
WAYS = FACES + CORNERS
ORDER = (7, 3, 5, 1, 0, 4, 6, 2)
HIGHEST = lax.Precision.HIGHEST


def lift_matrix(n):
    x = np.pad(np.eye(n), ((4, 4), (0, 0)), mode="reflect")
    e, o = x[0::2], x[1::2]
    d1 = o[:-1] + LIFT_ALPHA * (e[:-1] + e[1:])
    s1 = e[1:-1] + LIFT_BETA * (d1[:-1] + d1[1:])
    d2 = d1[1:-1] + LIFT_GAMMA * (s1[:-1] + s1[1:])
    s2 = s1[1:-1] + LIFT_DELTA * (d2[:-1] + d2[1:])
    return s2 * LIFT_SCALE, d2[1:] / LIFT_SCALE


def low_rank(coupling, rank):
    rest, us, vs = coupling.copy(), [], []
    for _ in range(rank):
        i, j = np.unravel_index(np.argmax(np.abs(rest)), rest.shape)
        u, v = rest[:, j] / rest[i, j], rest[i, :].copy()
        us.append(u)
        vs.append(v)
        rest = rest - u[:, None] * v[None, :]
    assert np.abs(rest).max() < 1e-12
    return np.stack(us, 1), np.stack(vs, 0)


def block_maps(b):
    blocks = 5
    low, high = lift_matrix(blocks * b)
    low2, high2 = lift_matrix(blocks * b // 2)
    pairs = ((low, high, 2), (low2 @ low, high2 @ low, 4))
    levels = []
    for lows, highs, rank in pairs:
        n = lows.shape[0] // blocks

        def part(row, col):
            cols = slice(col * b, (col + 1) * b)
            rows = slice(row * n, (row + 1) * n)
            return np.concatenate([lows[rows, cols], highs[rows, cols]])

        for row in range(blocks):
            for col in range(blocks):
                if abs(row - col) > 1:
                    assert np.abs(part(row, col)).max() == 0
                elif row != col:
                    like = part(2, 2 + col - row)
                    assert np.abs(part(row, col) - like).max() < 1e-12
        assert np.abs(part(1, 1) - part(2, 2)).max() < 1e-12
        assert np.abs(part(3, 3) - part(2, 2)).max() < 1e-12
        own = [part(0, 0), part(2, 2), part(4, 4)]
        u_up, v_up = low_rank(part(2, 1), rank)
        u_down, v_down = low_rank(part(2, 3), rank)
        levels.append((own, {1: u_up, -1: u_down}, {1: v_up, -1: v_down}))
    return levels


@functools.lru_cache(maxsize=None)
def tables(bx, by, nz):
    low, high = lift_matrix(nz)
    low2, high2 = lift_matrix(nz // 2)
    depth1 = np.concatenate([low, high]).T
    depth2 = np.concatenate([low2, high2]).T
    levels_x, levels_y = block_maps(bx), block_maps(by)
    own_x, ux, vx = levels_x[1]
    own_y, uy, vy = levels_y[1]
    nx, ny = own_x[0].shape[0], own_y[0].shape[0]
    plane = []
    for cx in range(3):
        for cy in range(3):
            out = []
            for dx, dy in WAYS:
                m = np.kron(vx[dx] if dx else own_x[cx], vy[dy] if dy else own_y[cy])
                if dx == 0:
                    m = m.reshape(nx, -1, bx * by).transpose(1, 0, 2).reshape(-1, bx * by)
                out.append(m)
            out.append(np.kron(own_x[cx], own_y[cy]))
            plane.append(np.concatenate(out))
    columns = np.concatenate([u[d].T.reshape(-1) for u in (levels_y[0][1], uy) for d in (1, -1)])
    columns = np.repeat(columns[:, None], 128, axis=1)
    arrays = [t.astype(np.float32) for t in (depth1, depth2, np.stack(plane), columns)]
    return arrays, levels_x, levels_y


def dot(a, b):
    return jnp.dot(a, b, precision=HIGHEST, preferred_element_type=jnp.float32)


def lift_ends(e, o, prev, after, first, last):
    at, sub = jnp.where, lambda f, *lists: [f(*v) for v in zip(*lists)]
    e_after = after(e, sub(lambda p: at(last, p, 0.0), e))
    d1 = sub(lambda p, q, r: p + LIFT_ALPHA * (q + r), o, e, e_after)
    out1 = sub(lambda p: LIFT_ALPHA * p, e)
    d1_prev = prev(d1, sub(lambda p, q: at(first, p, q), d1, out1))
    s1 = sub(lambda p, q, r: p + LIFT_BETA * (q + r), e, d1_prev, d1)
    s1_after = after(s1, sub(lambda p, q: at(last, p, LIFT_BETA * q), s1, d1))
    d2 = sub(lambda p, q, r: p + LIFT_GAMMA * (q + r), d1, s1, s1_after)
    out2 = sub(lambda p, q: p + LIFT_GAMMA * (LIFT_BETA * p + q), out1, s1)
    d2_prev = prev(d2, sub(lambda p, q: at(first, p, q), d2, out2))
    s2 = sub(lambda p, q, r: p + LIFT_DELTA * (q + r), s1, d2_prev, d2)
    return [v * LIFT_SCALE for v in s2], [v * (1.0 / LIFT_SCALE) for v in d2]


def weighted(weights, values):
    terms = [float(w) * v for w, v in zip(weights, values) if w != 0.0]
    return functools.reduce(lambda p, q: p + q, terms)


def kernel(
    nx, ny, levels_x, levels_y, x_hbm, t1_hbm, t2_hbm, s2_hbm, uy_hbm, approx, two, one,
    x_v, t1_v, t2_v, s2_v, uy_v, xb, own1,
    face1_out, face1_in, corner1_out, corner1_in, out2, in2,
    load_sem, send1, recv1, send2, recv2,
):
    px, py = lax.axis_index("slab"), lax.axis_index("morton")
    has_x = {1: jnp.minimum(nx - 1 - px, 1), -1: jnp.minimum(px, 1), 0: 1}
    has_y = {1: jnp.minimum(ny - 1 - py, 1), -1: jnp.minimum(py, 1), 0: 1}
    here = (has_x[-1] - has_x[1] + 1) * 3 + has_y[-1] - has_y[1] + 1

    def exists(dx, dy):
        return has_x[dx] * has_y[dy] == 1

    def rows(ref, start, size):
        return ref.at[pl.ds(start, size)]

    loads = [
        pltpu.make_async_copy(source, target, load_sem.at[k])
        for k, (source, target) in enumerate((
            (rows(x_hbm, 0, 8), rows(x_v, 0, 8)),
            (rows(t1_hbm, 0, 128), rows(t1_v, 0, 128)),
            (rows(x_hbm, 8, 8), rows(x_v, 8, 8)),
            (rows(t1_hbm, 128, 128), rows(t1_v, 128, 128)),
            (t2_hbm, t2_v),
            (s2_hbm.at[here], s2_v),
            (uy_hbm, uy_v),
        ))
    ]
    for load in loads:
        load.start()

    barrier = pltpu.get_barrier_semaphore()
    for dx, dy in WAYS:
        @pl.when(exists(dx, dy))
        def _():
            pl.semaphore_signal(
                barrier, inc=1, device_id=(py + dy, px + dx), device_id_type=MESH
            )

    def message(level, k):
        dx, dy = WAYS[k]
        if level == 1 and k < 4:
            pair = rows(face1_out, k * 32, 32), rows(face1_in, k * 32, 32)
        elif level == 1:
            pair = corner1_out.at[k - 4], corner1_in.at[k - 4]
        elif k < 4:
            pair = rows(out2, k * 32, 32), rows(in2, k * 32, 32)
        else:
            pair = rows(out2, 64 + k * 16, 16), rows(in2, 64 + k * 16, 16)
        send, recv = (send1, recv1) if level == 1 else (send2, recv2)
        return pltpu.make_async_remote_copy(
            src_ref=pair[0],
            dst_ref=pair[1],
            send_sem=send.at[k],
            recv_sem=recv.at[k],
            device_id=(py + dy, px + dx),
            device_id_type=MESH,
        )

    def start(level):
        for k in ORDER:
            @pl.when(exists(*WAYS[k]))
            def _():
                message(level, k).start()

    def receive(level):
        for k in ORDER:
            dx, dy = WAYS[k]

            @pl.when(exists(-dx, -dy))
            def _():
                message(level, k).wait_recv()

    for k, (dx, dy) in enumerate(WAYS):
        @pl.when(jnp.logical_not(exists(-dx, -dy)))
        def _():
            if k < 4:
                face1_in[k * 32:k * 32 + 32, :] = jnp.zeros((32, 256), jnp.float32)
                in2[k * 32:k * 32 + 32, :] = jnp.zeros((32, 128), jnp.float32)
            else:
                corner1_in[k - 4] = jnp.zeros((4, 256), jnp.float32)
                in2[64 + k * 16:80 + k * 16, :] = jnp.zeros((16, 128), jnp.float32)

    for load in loads[:4]:
        load.wait()
    z1 = dot(x_v[...].reshape(256, 256), t1_v[...])

    loads[4].wait()
    z2 = dot(z1[:, :128], t2_v[...])

    planes = [z1[16 * i:16 * i + 16, :] for i in range(16)]
    low, high = lift_ends(
        planes[0::2], planes[1::2],
        lambda v, end: [end[0]] + v[:-1],
        lambda v, end: v[1:] + [end[-1]],
        px == 0, px == nx - 1,
    )
    _, ux, vx = levels_x[0]
    _, uy, vy = levels_y[0]
    along = [weighted(w, planes) for d in (1, -1) for w in vx[d]]
    for r, v in enumerate(low + high + along):
        for h in range(2):
            xb[320 * h + 16 * r:320 * h + 16 * r + 16, :] = v[:, 128 * h:128 * h + 128]

    def strided(begin, size, stride):
        return jnp.concatenate(
            [xb[pl.ds(320 * h + begin, size, stride=stride), :] for h in range(2)], axis=1
        )

    for kd, d in enumerate((1, -1)):
        for ky in range(2):
            taps = [y for y in range(16) if vy[d][ky, y] != 0.0]
            weights = [vy[d][ky, y] for y in taps]
            at = (2 + kd) * 32 + ky * 16
            face1_out[at:at + 16, :] = weighted(
                weights, [strided(y, 16, 16) for y in taps]
            )
            part = weighted(weights, [strided(256 + y, 4, 16) for y in taps])
            corner1_out[kd, 2 * ky:2 * ky + 2, :] = part[0:2]
            corner1_out[2 + kd, 2 * ky:2 * ky + 2, :] = part[2:4]

    place = lax.broadcasted_iota(jnp.int32, (8, 256), 0)
    for r in (16, 17, 18, 19) + tuple(range(16)):
        low, high = lift_ends(
            [strided(16 * r, 8, 2)], [strided(16 * r + 1, 8, 2)],
            lambda v, end: [jnp.where(place == 0, end[0], pltpu.roll(v[0], 1, 0))],
            lambda v, end: [jnp.where(place == 7, end[0], pltpu.roll(v[0], 7, 0))],
            py == 0, py == ny - 1,
        )
        if r >= 16:
            at = (r - 16) * 16
            face1_out[at:at + 8, :] = low[0]
            face1_out[at + 8:at + 16, :] = high[0]
        else:
            own1[r, 0] = low[0]
            own1[r, 1] = high[0]
        if r == 19:
            pl.semaphore_wait(
                barrier,
                (1 + has_x[1] + has_x[-1]) * (1 + has_y[1] + has_y[-1]) - 1,
            )
            start(1)
            loads[5].wait()
            p2 = dot(s2_v[...], z2)
            out2[...] = p2[:192, :]
            start(2)
            own2 = p2[192:, :]

    loads[6].wait()

    receive(1)
    for bz in range(2):
        half = slice(bz * 128, bz * 128 + 128)
        column = [[[
            uy_v[((kd * 2 + ky) * 2 + b) * 8:((kd * 2 + ky) * 2 + b) * 8 + 8, :]
            for b in range(2)] for ky in range(2)] for kd in range(2)]

        def add_y(value, row, b):
            for kd in range(2):
                for ky in range(2):
                    value = value + row(kd, ky) * column[kd][ky][b]
            return value

        for b in range(2):
            side = [
                [
                    add_y(
                        face1_in[dx * 32 + kx * 16 + b * 8:dx * 32 + kx * 16 + b * 8 + 8, half],
                        lambda kd, ky: corner1_in[dx * 2 + kd, 2 * ky + kx:2 * ky + kx + 1, half],
                        b,
                    )
                    for kx in range(2)
                ]
                for dx in range(2)
            ]
            for r in range(16):
                band, i = 2 * (r // 8) + b, r % 8
                if band + bz == 0:
                    continue
                value = add_y(
                    own1[r, b, :, half],
                    lambda kd, ky: face1_in[
                        (2 + kd) * 32 + ky * 16 + r:(2 + kd) * 32 + ky * 16 + r + 1, half
                    ],
                    b,
                )
                for dx, d in enumerate((1, -1)):
                    if np.any(ux[d][r] != 0.0):
                        value = value + weighted(ux[d][r], side[dx])
                one[2 * band + bz - 1, i] = value

    for level in (1, 2):
        for k in ORDER:
            @pl.when(exists(*WAYS[k]))
            def _():
                message(level, k).wait_send()

    receive(2)
    _, ux2, _ = levels_x[1]
    column2 = [uy_v[64 + k * 8:72 + k * 8, :] for k in range(8)]
    side2 = [
        [
            in2[dx * 32 + kx * 8:dx * 32 + kx * 8 + 8, :]
            + sum(
                in2[at:at + 1, :] * column2[kd * 4 + ky]
                for kd in range(2)
                for ky in range(4)
                for at in (128 + (dx * 2 + kd) * 16 + kx * 4 + ky,)
            )
            for kx in range(4)
        ]
        for dx in range(2)
    ]
    for r in range(8):
        value = own2[r * 8:r * 8 + 8, :] + sum(
            in2[at:at + 1, :] * column2[kd * 4 + ky]
            for kd in range(2)
            for ky in range(4)
            for at in ((2 + kd) * 32 + ky * 8 + r,)
        )
        for dx, d in enumerate((1, -1)):
            if np.any(ux2[d][r] != 0.0):
                value = value + weighted(ux2[d][r], side2[dx])
        for b in range(2):
            for bz in range(2):
                at, part = 4 * (r // 4) + 2 * b + bz, value[4 * b:4 * b + 4, 64 * bz:64 * bz + 64]
                if at:
                    two[at - 1, r % 4] = part
                else:
                    approx[r % 4] = part


def store(approx_v, two_v, one_v, approx, two, one, sem):
    pairs = ((one_v, one), (two_v, two), (approx_v, approx))
    copies = [pltpu.make_async_copy(a, b, sem.at[k]) for k, (a, b) in enumerate(pairs)]
    for copy in copies:
        copy.start()
    for copy in copies:
        copy.wait()


def per_device(nx, ny, velocity):
    bx, by, nz = velocity.shape
    consts, levels_x, levels_y = tables(bx, by, nz)
    f32 = jnp.float32
    vmem = pl.BlockSpec(memory_space=pltpu.VMEM)
    held = [pltpu.VMEM(c.shape[-2:], f32) for c in consts]
    shapes = (
        (bx // 4, by // 4, nz // 4),
        (7, bx // 4, by // 4, nz // 4),
        (7, bx // 2, by // 2, nz // 2),
    )
    results = pl.pallas_call(
        functools.partial(kernel, nx, ny, levels_x, levels_y),
        out_shape=tuple(pltpu.VMEM(shape, f32) for shape in shapes),
        in_specs=[pl.BlockSpec(memory_space=pl.ANY)] * 5,
        out_specs=(vmem, vmem, vmem),
        scratch_shapes=[pltpu.VMEM((bx, by, nz), f32)]
        + held
        + [
            pltpu.VMEM((640, 128), f32),
            pltpu.VMEM((16, 2, 8, 256), f32),
            pltpu.VMEM((128, 256), f32),
            pltpu.VMEM((128, 256), f32),
            pltpu.VMEM((4, 4, 256), f32),
            pltpu.VMEM((4, 4, 256), f32),
            pltpu.VMEM((192, 128), f32),
            pltpu.VMEM((192, 128), f32),
            pltpu.SemaphoreType.DMA((7,)),
        ]
        + [pltpu.SemaphoreType.DMA((8,))] * 4,
        compiler_params=pltpu.CompilerParams(
            collective_id=0, has_side_effects=True, vmem_limit_bytes=60 * 1024 * 1024
        ),
    )(velocity, *[jnp.asarray(c) for c in consts])
    results = [pltpu.with_memory_space_constraint(r, pltpu.VMEM) for r in results]
    return pl.pallas_call(
        store,
        out_shape=tuple(jax.ShapeDtypeStruct(shape, f32) for shape in shapes),
        in_specs=[vmem] * 3,
        out_specs=[pl.BlockSpec(memory_space=pl.ANY)] * 3,
        scratch_shapes=[pltpu.SemaphoreType.DMA((3,))],
    )(*results)


def solution(mesh):
    placed = (P("slab", "morton", None),)
    return jax.shard_map(
        functools.partial(per_device, mesh.shape["slab"], mesh.shape["morton"]),
        mesh=mesh,
        in_specs=placed,
        out_specs=(
            P("slab", "morton", None),
            P(None, "slab", "morton", None),
            P(None, "slab", "morton", None),
        ),
        check_vma=False,
    )
```

```python
import functools

import jax
import jax.numpy as jnp
import numpy as np
from jax import lax
from jax.experimental import pallas as pl
from jax.experimental.pallas import tpu as pltpu
from jax.sharding import PartitionSpec as P

LIFT_ALPHA = -1.586134342059924
LIFT_BETA = -0.052980118572961
LIFT_GAMMA = 0.882911075530934
LIFT_DELTA = 0.443506852043971
LIFT_SCALE = 1.149604398860241

MESH = pl.DeviceIdType.MESH
FACES = ((1, 0), (-1, 0), (0, 1), (0, -1))
CORNERS = ((1, 1), (1, -1), (-1, 1), (-1, -1))
WAYS = FACES + CORNERS
ORDER = (7, 3, 5, 1, 0, 4, 6, 2)
HIGHEST = lax.Precision.HIGHEST


def lift_matrix(n):
    x = np.pad(np.eye(n), ((4, 4), (0, 0)), mode="reflect")
    e, o = x[0::2], x[1::2]
    d1 = o[:-1] + LIFT_ALPHA * (e[:-1] + e[1:])
    s1 = e[1:-1] + LIFT_BETA * (d1[:-1] + d1[1:])
    d2 = d1[1:-1] + LIFT_GAMMA * (s1[:-1] + s1[1:])
    s2 = s1[1:-1] + LIFT_DELTA * (d2[:-1] + d2[1:])
    return s2 * LIFT_SCALE, d2[1:] / LIFT_SCALE


def low_rank(coupling, rank):
    rest, us, vs = coupling.copy(), [], []
    for _ in range(rank):
        i, j = np.unravel_index(np.argmax(np.abs(rest)), rest.shape)
        u, v = rest[:, j] / rest[i, j], rest[i, :].copy()
        us.append(u)
        vs.append(v)
        rest = rest - u[:, None] * v[None, :]
    assert np.abs(rest).max() < 1e-12
    return np.stack(us, 1), np.stack(vs, 0)


def block_maps(b):
    blocks = 5
    low, high = lift_matrix(blocks * b)
    low2, high2 = lift_matrix(blocks * b // 2)
    pairs = ((low, high, 2), (low2 @ low, high2 @ low, 4))
    levels = []
    for lows, highs, rank in pairs:
        n = lows.shape[0] // blocks

        def part(row, col):
            cols = slice(col * b, (col + 1) * b)
            rows = slice(row * n, (row + 1) * n)
            return np.concatenate([lows[rows, cols], highs[rows, cols]])

        for row in range(blocks):
            for col in range(blocks):
                if abs(row - col) > 1:
                    assert np.abs(part(row, col)).max() == 0
                elif row != col:
                    like = part(2, 2 + col - row)
                    assert np.abs(part(row, col) - like).max() < 1e-12
        assert np.abs(part(1, 1) - part(2, 2)).max() < 1e-12
        assert np.abs(part(3, 3) - part(2, 2)).max() < 1e-12
        own = [part(0, 0), part(2, 2), part(4, 4)]
        u_up, v_up = low_rank(part(2, 1), rank)
        u_down, v_down = low_rank(part(2, 3), rank)
        levels.append((own, {1: u_up, -1: u_down}, {1: v_up, -1: v_down}))
    return levels


@functools.lru_cache(maxsize=None)
def tables(bx, by, nz):
    low, high = lift_matrix(nz)
    low2, high2 = lift_matrix(nz // 2)
    depth1 = np.concatenate([low, high]).T
    depth2 = np.concatenate([low2 @ low, high2 @ low]).T
    levels_x, levels_y = block_maps(bx), block_maps(by)
    own_x, ux, vx = levels_x[1]
    own_y, uy, vy = levels_y[1]
    nx, ny = own_x[0].shape[0], own_y[0].shape[0]
    plane = []
    for cx in range(3):
        for cy in range(3):
            out = []
            for dx, dy in WAYS:
                m = np.kron(vx[dx] if dx else own_x[cx], vy[dy] if dy else own_y[cy])
                if dx == 0:
                    m = m.reshape(nx, -1, bx * by).transpose(1, 0, 2).reshape(-1, bx * by)
                out.append(m)
            out.append(np.kron(own_x[cx], own_y[cy]))
            plane.append(np.concatenate(out))
    columns = np.concatenate([u[d].T.reshape(-1) for u in (levels_y[0][1], uy) for d in (1, -1)])
    columns = np.repeat(columns[:, None], 128, axis=1)
    arrays = [t.astype(np.float32) for t in (depth1, depth2, np.stack(plane), columns)]
    return arrays, levels_x, levels_y


def dot(a, b):
    return jnp.dot(a, b, precision=HIGHEST, preferred_element_type=jnp.float32)


def lift_ends(e, o, prev, after, first, last):
    at, sub = jnp.where, lambda f, *lists: [f(*v) for v in zip(*lists)]
    e_after = after(e, sub(lambda p: at(last, p, 0.0), e))
    d1 = sub(lambda p, q, r: p + LIFT_ALPHA * (q + r), o, e, e_after)
    out1 = sub(lambda p: LIFT_ALPHA * p, e)
    d1_prev = prev(d1, sub(lambda p, q: at(first, p, q), d1, out1))
    s1 = sub(lambda p, q, r: p + LIFT_BETA * (q + r), e, d1_prev, d1)
    s1_after = after(s1, sub(lambda p, q: at(last, p, LIFT_BETA * q), s1, d1))
    d2 = sub(lambda p, q, r: p + LIFT_GAMMA * (q + r), d1, s1, s1_after)
    out2 = sub(lambda p, q: p + LIFT_GAMMA * (LIFT_BETA * p + q), out1, s1)
    d2_prev = prev(d2, sub(lambda p, q: at(first, p, q), d2, out2))
    s2 = sub(lambda p, q, r: p + LIFT_DELTA * (q + r), s1, d2_prev, d2)
    return [v * LIFT_SCALE for v in s2], [v * (1.0 / LIFT_SCALE) for v in d2]


def weighted(weights, values):
    terms = [float(w) * v for w, v in zip(weights, values) if w != 0.0]
    return functools.reduce(lambda p, q: p + q, terms)


def kernel(
    nx, ny, levels_x, levels_y, x_hbm, t1_hbm, t2_hbm, s2_hbm, uy_hbm, approx, two, one,
    x_v, t1_v, t2_v, s2_v, uy_v, xb, own1, full,
    face1_out, face1_in, corner1_out, corner1_in, out2, in2,
    load_sem, send1, recv1, send2, recv2,
):
    px, py = lax.axis_index("slab"), lax.axis_index("morton")
    has_x = {1: jnp.minimum(nx - 1 - px, 1), -1: jnp.minimum(px, 1), 0: 1}
    has_y = {1: jnp.minimum(ny - 1 - py, 1), -1: jnp.minimum(py, 1), 0: 1}
    here = (has_x[-1] - has_x[1] + 1) * 3 + has_y[-1] - has_y[1] + 1

    def exists(dx, dy):
        return has_x[dx] * has_y[dy] == 1

    def rows(ref, start, size):
        return ref.at[pl.ds(start, size)]

    loads = [
        pltpu.make_async_copy(source, target, load_sem.at[k])
        for k, (source, target) in enumerate((
            (x_hbm, x_v),
            (t2_hbm, t2_v),
            (s2_hbm.at[here], s2_v),
            (uy_hbm, uy_v),
            (t1_hbm, t1_v),
        ))
    ]
    for load in loads:
        load.start()

    barrier = pltpu.get_barrier_semaphore()
    for dx, dy in WAYS:
        @pl.when(exists(dx, dy))
        def _():
            pl.semaphore_signal(
                barrier, inc=1, device_id=(py + dy, px + dx), device_id_type=MESH
            )

    def message(level, k):
        dx, dy = WAYS[k]
        if level == 1 and k < 4:
            pair = rows(face1_out, k * 32, 32), rows(face1_in, k * 32, 32)
        elif level == 1:
            pair = corner1_out.at[k - 4], corner1_in.at[k - 4]
        elif k < 4:
            pair = rows(out2, k * 32, 32), rows(in2, k * 32, 32)
        else:
            pair = rows(out2, 64 + k * 16, 16), rows(in2, 64 + k * 16, 16)
        send, recv = (send1, recv1) if level == 1 else (send2, recv2)
        return pltpu.make_async_remote_copy(
            src_ref=pair[0],
            dst_ref=pair[1],
            send_sem=send.at[k],
            recv_sem=recv.at[k],
            device_id=(py + dy, px + dx),
            device_id_type=MESH,
        )

    def start(level):
        for k in ORDER:
            @pl.when(exists(*WAYS[k]))
            def _():
                message(level, k).start()

    def receive(level):
        for k in ORDER:
            dx, dy = WAYS[k]

            @pl.when(exists(-dx, -dy))
            def _():
                message(level, k).wait_recv()

    for k, (dx, dy) in enumerate(WAYS):
        @pl.when(jnp.logical_not(exists(-dx, -dy)))
        def _():
            if k < 4:
                face1_in[k * 32:k * 32 + 32, :] = jnp.zeros((32, 256), jnp.float32)
                in2[k * 32:k * 32 + 32, :] = jnp.zeros((32, 128), jnp.float32)
            else:
                corner1_in[k - 4] = jnp.zeros((4, 256), jnp.float32)
                in2[64 + k * 16:80 + k * 16, :] = jnp.zeros((16, 128), jnp.float32)

    loads[0].wait()

    planes = [x_v[i] for i in range(16)]
    low, high = lift_ends(
        planes[0::2], planes[1::2],
        lambda v, end: [end[0]] + v[:-1],
        lambda v, end: v[1:] + [end[-1]],
        px == 0, px == nx - 1,
    )
    _, ux, vx = levels_x[0]
    _, uy, vy = levels_y[0]
    along = [weighted(w, planes) for d in (1, -1) for w in vx[d]]
    for r, v in enumerate(low + high + along):
        for h in range(2):
            xb[320 * h + 16 * r:320 * h + 16 * r + 16, :] = v[:, 128 * h:128 * h + 128]

    def strided(begin, size, stride):
        return jnp.concatenate(
            [xb[pl.ds(320 * h + begin, size, stride=stride), :] for h in range(2)], axis=1
        )

    for kd, d in enumerate((1, -1)):
        for ky in range(2):
            taps = [y for y in range(16) if vy[d][ky, y] != 0.0]
            weights = [vy[d][ky, y] for y in taps]
            at = (2 + kd) * 32 + ky * 16
            face1_out[at:at + 16, :] = weighted(
                weights, [strided(y, 16, 16) for y in taps]
            )
            part = weighted(weights, [strided(256 + y, 4, 16) for y in taps])
            corner1_out[kd, 2 * ky:2 * ky + 2, :] = part[0:2]
            corner1_out[2 + kd, 2 * ky:2 * ky + 2, :] = part[2:4]

    place = lax.broadcasted_iota(jnp.int32, (8, 256), 0)
    for r in (16, 17, 18, 19) + tuple(range(16)):
        low, high = lift_ends(
            [strided(16 * r, 8, 2)], [strided(16 * r + 1, 8, 2)],
            lambda v, end: [jnp.where(place == 0, end[0], pltpu.roll(v[0], 1, 0))],
            lambda v, end: [jnp.where(place == 7, end[0], pltpu.roll(v[0], 7, 0))],
            py == 0, py == ny - 1,
        )
        if r >= 16:
            at = (r - 16) * 16
            face1_out[at:at + 8, :] = low[0]
            face1_out[at + 8:at + 16, :] = high[0]
        else:
            own1[r, 0] = low[0]
            own1[r, 1] = high[0]
        if r == 19:
            pl.semaphore_wait(
                barrier,
                (1 + has_x[1] + has_x[-1]) * (1 + has_y[1] + has_y[-1]) - 1,
            )
            start(1)

    loads[1].wait()
    z2 = dot(x_v[...].reshape(256, 256), t2_v[...])
    loads[2].wait()
    p2 = dot(s2_v[...], z2)
    out2[...] = p2[:192, :]
    start(2)
    own2 = p2[192:, :]
    loads[3].wait()
    loads[4].wait()

    receive(1)
    for bz in range(2):
        half = slice(bz * 128, bz * 128 + 128)
        column = [[[
            uy_v[((kd * 2 + ky) * 2 + b) * 8:((kd * 2 + ky) * 2 + b) * 8 + 8, :]
            for b in range(2)] for ky in range(2)] for kd in range(2)]

        def add_y(value, row, b):
            for kd in range(2):
                for ky in range(2):
                    value = value + row(kd, ky) * column[kd][ky][b]
            return value

        for b in range(2):
            side = [
                [
                    add_y(
                        face1_in[dx * 32 + kx * 16 + b * 8:dx * 32 + kx * 16 + b * 8 + 8, half],
                        lambda kd, ky: corner1_in[dx * 2 + kd, 2 * ky + kx:2 * ky + kx + 1, half],
                        b,
                    )
                    for kx in range(2)
                ]
                for dx in range(2)
            ]
            for r in range(16):
                band, i = 2 * (r // 8) + b, r % 8
                value = add_y(
                    own1[r, b, :, half],
                    lambda kd, ky: face1_in[
                        (2 + kd) * 32 + ky * 16 + r:(2 + kd) * 32 + ky * 16 + r + 1, half
                    ],
                    b,
                )
                for dx, d in enumerate((1, -1)):
                    if np.any(ux[d][r] != 0.0):
                        value = value + weighted(ux[d][r], side[dx])
                full[band * 64 + i * 8:band * 64 + i * 8 + 8, half] = value

    o1 = dot(full[...], t1_v[...])
    for band in range(4):
        for bz in range(2):
            if band + bz:
                one[2 * band + bz - 1] = o1[
                    band * 64:band * 64 + 64, bz * 128:bz * 128 + 128
                ].reshape(8, 8, 128)

    for level in (1, 2):
        for k in ORDER:
            @pl.when(exists(*WAYS[k]))
            def _():
                message(level, k).wait_send()

    receive(2)
    _, ux2, _ = levels_x[1]
    column2 = [uy_v[64 + k * 8:72 + k * 8, :] for k in range(8)]
    side2 = [
        [
            in2[dx * 32 + kx * 8:dx * 32 + kx * 8 + 8, :]
            + sum(
                in2[at:at + 1, :] * column2[kd * 4 + ky]
                for kd in range(2)
                for ky in range(4)
                for at in (128 + (dx * 2 + kd) * 16 + kx * 4 + ky,)
            )
            for kx in range(4)
        ]
        for dx in range(2)
    ]
    for r in range(8):
        value = own2[r * 8:r * 8 + 8, :] + sum(
            in2[at:at + 1, :] * column2[kd * 4 + ky]
            for kd in range(2)
            for ky in range(4)
            for at in ((2 + kd) * 32 + ky * 8 + r,)
        )
        for dx, d in enumerate((1, -1)):
            if np.any(ux2[d][r] != 0.0):
                value = value + weighted(ux2[d][r], side2[dx])
        for b in range(2):
            for bz in range(2):
                at, part = 4 * (r // 4) + 2 * b + bz, value[4 * b:4 * b + 4, 64 * bz:64 * bz + 64]
                if at:
                    two[at - 1, r % 4] = part
                else:
                    approx[r % 4] = part


def store(approx_v, two_v, one_v, approx, two, one, sem):
    pairs = ((one_v, one), (two_v, two), (approx_v, approx))
    copies = [pltpu.make_async_copy(a, b, sem.at[k]) for k, (a, b) in enumerate(pairs)]
    for copy in copies:
        copy.start()
    for copy in copies:
        copy.wait()


def per_device(nx, ny, velocity):
    bx, by, nz = velocity.shape
    consts, levels_x, levels_y = tables(bx, by, nz)
    f32 = jnp.float32
    vmem = pl.BlockSpec(memory_space=pltpu.VMEM)
    held = [pltpu.VMEM(c.shape[-2:], f32) for c in consts]
    shapes = (
        (bx // 4, by // 4, nz // 4),
        (7, bx // 4, by // 4, nz // 4),
        (7, bx // 2, by // 2, nz // 2),
    )
    results = pl.pallas_call(
        functools.partial(kernel, nx, ny, levels_x, levels_y),
        out_shape=tuple(pltpu.VMEM(shape, f32) for shape in shapes),
        in_specs=[pl.BlockSpec(memory_space=pl.ANY)] * 5,
        out_specs=(vmem, vmem, vmem),
        scratch_shapes=[pltpu.VMEM((bx, by, nz), f32)]
        + held
        + [
            pltpu.VMEM((640, 128), f32),
            pltpu.VMEM((16, 2, 8, 256), f32),
            pltpu.VMEM((256, 256), f32),
            pltpu.VMEM((128, 256), f32),
            pltpu.VMEM((128, 256), f32),
            pltpu.VMEM((4, 4, 256), f32),
            pltpu.VMEM((4, 4, 256), f32),
            pltpu.VMEM((192, 128), f32),
            pltpu.VMEM((192, 128), f32),
            pltpu.SemaphoreType.DMA((5,)),
        ]
        + [pltpu.SemaphoreType.DMA((8,))] * 4,
        compiler_params=pltpu.CompilerParams(
            collective_id=0, has_side_effects=True, vmem_limit_bytes=60 * 1024 * 1024
        ),
    )(velocity, *[jnp.asarray(c) for c in consts])
    results = [pltpu.with_memory_space_constraint(r, pltpu.VMEM) for r in results]
    return pl.pallas_call(
        store,
        out_shape=tuple(jax.ShapeDtypeStruct(shape, f32) for shape in shapes),
        in_specs=[vmem] * 3,
        out_specs=[pl.BlockSpec(memory_space=pl.ANY)] * 3,
        scratch_shapes=[pltpu.SemaphoreType.DMA((3,))],
    )(*results)


def solution(mesh):
    placed = (P("slab", "morton", None),)
    return jax.shard_map(
        functools.partial(per_device, mesh.shape["slab"], mesh.shape["morton"]),
        mesh=mesh,
        in_specs=placed,
        out_specs=(
            P("slab", "morton", None),
            P(None, "slab", "morton", None),
            P(None, "slab", "morton", None),
        ),
        check_vma=False,
    )
```

```python
import functools

import jax
import jax.numpy as jnp
import numpy as np
from jax import lax
from jax.experimental import pallas as pl
from jax.experimental.pallas import tpu as pltpu
from jax.sharding import PartitionSpec as P

LIFT_ALPHA = -1.586134342059924
LIFT_BETA = -0.052980118572961
LIFT_GAMMA = 0.882911075530934
LIFT_DELTA = 0.443506852043971
LIFT_SCALE = 1.149604398860241

MESH = pl.DeviceIdType.MESH
FACES = ((1, 0), (-1, 0), (0, 1), (0, -1))
CORNERS = ((1, 1), (1, -1), (-1, 1), (-1, -1))
WAYS = FACES + CORNERS
ORDER = (7, 3, 5, 1, 0, 4, 6, 2)
HIGHEST = lax.Precision.HIGHEST


def lift_matrix(n):
    x = np.pad(np.eye(n), ((4, 4), (0, 0)), mode="reflect")
    e, o = x[0::2], x[1::2]
    d1 = o[:-1] + LIFT_ALPHA * (e[:-1] + e[1:])
    s1 = e[1:-1] + LIFT_BETA * (d1[:-1] + d1[1:])
    d2 = d1[1:-1] + LIFT_GAMMA * (s1[:-1] + s1[1:])
    s2 = s1[1:-1] + LIFT_DELTA * (d2[:-1] + d2[1:])
    return s2 * LIFT_SCALE, d2[1:] / LIFT_SCALE


def low_rank(coupling, rank):
    rest, us, vs = coupling.copy(), [], []
    for _ in range(rank):
        i, j = np.unravel_index(np.argmax(np.abs(rest)), rest.shape)
        u, v = rest[:, j] / rest[i, j], rest[i, :].copy()
        us.append(u)
        vs.append(v)
        rest = rest - u[:, None] * v[None, :]
    assert np.abs(rest).max() < 1e-12
    return np.stack(us, 1), np.stack(vs, 0)


def block_maps(b):
    blocks = 5
    low, high = lift_matrix(blocks * b)
    low2, high2 = lift_matrix(blocks * b // 2)
    pairs = ((low, high, 2), (low2 @ low, high2 @ low, 4))
    levels = []
    for lows, highs, rank in pairs:
        n = lows.shape[0] // blocks

        def part(row, col):
            cols = slice(col * b, (col + 1) * b)
            rows = slice(row * n, (row + 1) * n)
            return np.concatenate([lows[rows, cols], highs[rows, cols]])

        for row in range(blocks):
            for col in range(blocks):
                if abs(row - col) > 1:
                    assert np.abs(part(row, col)).max() == 0
                elif row != col:
                    like = part(2, 2 + col - row)
                    assert np.abs(part(row, col) - like).max() < 1e-12
        assert np.abs(part(1, 1) - part(2, 2)).max() < 1e-12
        assert np.abs(part(3, 3) - part(2, 2)).max() < 1e-12
        own = [part(0, 0), part(2, 2), part(4, 4)]
        u_up, v_up = low_rank(part(2, 1), rank)
        u_down, v_down = low_rank(part(2, 3), rank)
        levels.append((own, {1: u_up, -1: u_down}, {1: v_up, -1: v_down}))
    return levels


@functools.lru_cache(maxsize=None)
def tables(bx, by, nz):
    low, high = lift_matrix(nz)
    low2, high2 = lift_matrix(nz // 2)
    depth1 = np.concatenate([low, high]).T
    depth2 = np.concatenate([low2, high2]).T
    levels_x, levels_y = block_maps(bx), block_maps(by)
    own_x, ux, vx = levels_x[1]
    own_y, uy, vy = levels_y[1]
    nx, ny = own_x[0].shape[0], own_y[0].shape[0]
    plane = []
    for cx in range(3):
        for cy in range(3):
            out = []
            for dx, dy in WAYS:
                m = np.kron(vx[dx] if dx else own_x[cx], vy[dy] if dy else own_y[cy])
                if dx == 0:
                    m = m.reshape(nx, -1, bx * by).transpose(1, 0, 2).reshape(-1, bx * by)
                out.append(m)
            out.append(np.kron(own_x[cx], own_y[cy]))
            plane.append(np.concatenate(out))
    columns = np.concatenate([u[d].T.reshape(-1) for u in (levels_y[0][1], uy) for d in (1, -1)])
    columns = np.repeat(columns[:, None], 128, axis=1)
    arrays = [t.astype(np.float32) for t in (depth1, depth2, np.stack(plane), columns)]
    return arrays, levels_x, levels_y


def dot(a, b):
    return jnp.dot(a, b, precision=HIGHEST, preferred_element_type=jnp.float32)


def lift_ends(e, o, prev, after, first, last):
    at, sub = jnp.where, lambda f, *lists: [f(*v) for v in zip(*lists)]
    e_after = after(e, sub(lambda p: at(last, p, 0.0), e))
    d1 = sub(lambda p, q, r: p + LIFT_ALPHA * (q + r), o, e, e_after)
    out1 = sub(lambda p: LIFT_ALPHA * p, e)
    d1_prev = prev(d1, sub(lambda p, q: at(first, p, q), d1, out1))
    s1 = sub(lambda p, q, r: p + LIFT_BETA * (q + r), e, d1_prev, d1)
    s1_after = after(s1, sub(lambda p, q: at(last, p, LIFT_BETA * q), s1, d1))
    d2 = sub(lambda p, q, r: p + LIFT_GAMMA * (q + r), d1, s1, s1_after)
    out2 = sub(lambda p, q: p + LIFT_GAMMA * (LIFT_BETA * p + q), out1, s1)
    d2_prev = prev(d2, sub(lambda p, q: at(first, p, q), d2, out2))
    s2 = sub(lambda p, q, r: p + LIFT_DELTA * (q + r), s1, d2_prev, d2)
    return [v * LIFT_SCALE for v in s2], [v * (1.0 / LIFT_SCALE) for v in d2]


def weighted(weights, values):
    terms = [float(w) * v for w, v in zip(weights, values) if w != 0.0]
    return functools.reduce(lambda p, q: p + q, terms)


def kernel(
    nx, ny, levels_x, levels_y, x_hbm, t1_hbm, t2_hbm, s2_hbm, uy_hbm, approx, two, one,
    x_v, t1_v, t2_v, s2_v, uy_v, xb, own1,
    face1_out, face1_in, corner1_out, corner1_in, out2, in2,
    load_sem, send1, recv1, send2, recv2,
):
    px, py = lax.axis_index("slab"), lax.axis_index("morton")
    has_x = {1: jnp.minimum(nx - 1 - px, 1), -1: jnp.minimum(px, 1), 0: 1}
    has_y = {1: jnp.minimum(ny - 1 - py, 1), -1: jnp.minimum(py, 1), 0: 1}
    here = (has_x[-1] - has_x[1] + 1) * 3 + has_y[-1] - has_y[1] + 1

    def exists(dx, dy):
        return has_x[dx] * has_y[dy] == 1

    def rows(ref, start, size):
        return ref.at[pl.ds(start, size)]

    loads = [
        pltpu.make_async_copy(source, target, load_sem.at[k])
        for k, (source, target) in enumerate((
            (rows(x_hbm, 0, 8), rows(x_v, 0, 8)),
            (rows(t1_hbm, 0, 128), rows(t1_v, 0, 128)),
            (rows(x_hbm, 8, 8), rows(x_v, 8, 8)),
            (rows(t1_hbm, 128, 128), rows(t1_v, 128, 128)),
            (t2_hbm, t2_v),
            (s2_hbm.at[here], s2_v),
            (uy_hbm, uy_v),
        ))
    ]
    for load in loads:
        load.start()

    barrier = pltpu.get_barrier_semaphore()
    for dx, dy in WAYS:
        @pl.when(exists(dx, dy))
        def _():
            pl.semaphore_signal(
                barrier, inc=1, device_id=(py + dy, px + dx), device_id_type=MESH
            )

    def message(level, k):
        dx, dy = WAYS[k]
        if level == 1 and k < 4:
            pair = rows(face1_out, k * 32, 32), rows(face1_in, k * 32, 32)
        elif level == 1:
            pair = corner1_out.at[k - 4], corner1_in.at[k - 4]
        elif k < 4:
            pair = rows(out2, k * 32, 32), rows(in2, k * 32, 32)
        else:
            pair = rows(out2, 64 + k * 16, 16), rows(in2, 64 + k * 16, 16)
        send, recv = (send1, recv1) if level == 1 else (send2, recv2)
        return pltpu.make_async_remote_copy(
            src_ref=pair[0],
            dst_ref=pair[1],
            send_sem=send.at[k],
            recv_sem=recv.at[k],
            device_id=(py + dy, px + dx),
            device_id_type=MESH,
        )

    def start(level, ways=ORDER):
        for k in ways:
            @pl.when(exists(*WAYS[k]))
            def _():
                message(level, k).start()

    def receive(level):
        for k in ORDER:
            dx, dy = WAYS[k]

            @pl.when(exists(-dx, -dy))
            def _():
                message(level, k).wait_recv()

    for k, (dx, dy) in enumerate(WAYS):
        @pl.when(jnp.logical_not(exists(-dx, -dy)))
        def _():
            if k < 4:
                face1_in[k * 32:k * 32 + 32, :] = jnp.zeros((32, 256), jnp.float32)
                in2[k * 32:k * 32 + 32, :] = jnp.zeros((32, 128), jnp.float32)
            else:
                corner1_in[k - 4] = jnp.zeros((4, 256), jnp.float32)
                in2[64 + k * 16:80 + k * 16, :] = jnp.zeros((16, 128), jnp.float32)

    for load in loads[:4]:
        load.wait()
    z1 = dot(x_v[...].reshape(256, 256), t1_v[...])

    planes = [z1[16 * i:16 * i + 16, :] for i in range(16)]
    low, high = lift_ends(
        planes[0::2], planes[1::2],
        lambda v, end: [end[0]] + v[:-1],
        lambda v, end: v[1:] + [end[-1]],
        px == 0, px == nx - 1,
    )
    _, ux, vx = levels_x[0]
    _, uy, vy = levels_y[0]
    along = [weighted(w, planes) for d in (1, -1) for w in vx[d]]
    for r, v in enumerate(low + high + along):
        for h in range(2):
            xb[320 * h + 16 * r:320 * h + 16 * r + 16, :] = v[:, 128 * h:128 * h + 128]

    def strided(begin, size, stride):
        return jnp.concatenate(
            [xb[pl.ds(320 * h + begin, size, stride=stride), :] for h in range(2)], axis=1
        )

    for kd, d in enumerate((1, -1)):
        for ky in range(2):
            taps = [y for y in range(16) if vy[d][ky, y] != 0.0]
            weights = [vy[d][ky, y] for y in taps]
            at = (2 + kd) * 32 + ky * 16
            face1_out[at:at + 16, :] = weighted(
                weights, [strided(y, 16, 16) for y in taps]
            )
            part = weighted(weights, [strided(256 + y, 4, 16) for y in taps])
            corner1_out[kd, 2 * ky:2 * ky + 2, :] = part[0:2]
            corner1_out[2 + kd, 2 * ky:2 * ky + 2, :] = part[2:4]

    pl.semaphore_wait(
        barrier,
        (1 + has_x[1] + has_x[-1]) * (1 + has_y[1] + has_y[-1]) - 1,
    )
    start(1, [k for k in ORDER if WAYS[k][1]])

    place = lax.broadcasted_iota(jnp.int32, (8, 256), 0)
    for r in (16, 17, 18, 19) + tuple(range(16)):
        low, high = lift_ends(
            [strided(16 * r, 8, 2)], [strided(16 * r + 1, 8, 2)],
            lambda v, end: [jnp.where(place == 0, end[0], pltpu.roll(v[0], 1, 0))],
            lambda v, end: [jnp.where(place == 7, end[0], pltpu.roll(v[0], 7, 0))],
            py == 0, py == ny - 1,
        )
        if r >= 16:
            at = (r - 16) * 16
            face1_out[at:at + 8, :] = low[0]
            face1_out[at + 8:at + 16, :] = high[0]
        else:
            own1[r, 0] = low[0]
            own1[r, 1] = high[0]
        if r == 19:
            start(1, [k for k in ORDER if not WAYS[k][1]])

    loads[4].wait()
    z2 = dot(z1[:, :128], t2_v[...])
    loads[5].wait()
    p2 = dot(s2_v[...], z2)
    out2[...] = p2[:192, :]
    start(2)
    own2 = p2[192:, :]
    loads[6].wait()

    receive(1)
    for bz in range(2):
        half = slice(bz * 128, bz * 128 + 128)
        column = [[[
            uy_v[((kd * 2 + ky) * 2 + b) * 8:((kd * 2 + ky) * 2 + b) * 8 + 8, :]
            for b in range(2)] for ky in range(2)] for kd in range(2)]

        def add_y(value, row, b):
            for kd in range(2):
                for ky in range(2):
                    value = value + row(kd, ky) * column[kd][ky][b]
            return value

        for b in range(2):
            side = [
                [
                    add_y(
                        face1_in[dx * 32 + kx * 16 + b * 8:dx * 32 + kx * 16 + b * 8 + 8, half],
                        lambda kd, ky: corner1_in[dx * 2 + kd, 2 * ky + kx:2 * ky + kx + 1, half],
                        b,
                    )
                    for kx in range(2)
                ]
                for dx in range(2)
            ]
            for r in range(16):
                band, i = 2 * (r // 8) + b, r % 8
                if band + bz == 0:
                    continue
                value = add_y(
                    own1[r, b, :, half],
                    lambda kd, ky: face1_in[
                        (2 + kd) * 32 + ky * 16 + r:(2 + kd) * 32 + ky * 16 + r + 1, half
                    ],
                    b,
                )
                for dx, d in enumerate((1, -1)):
                    if np.any(ux[d][r] != 0.0):
                        value = value + weighted(ux[d][r], side[dx])
                one[2 * band + bz - 1, i] = value

    for level in (1, 2):
        for k in ORDER:
            @pl.when(exists(*WAYS[k]))
            def _():
                message(level, k).wait_send()

    receive(2)
    _, ux2, _ = levels_x[1]
    column2 = [uy_v[64 + k * 8:72 + k * 8, :] for k in range(8)]
    side2 = [
        [
            in2[dx * 32 + kx * 8:dx * 32 + kx * 8 + 8, :]
            + sum(
                in2[at:at + 1, :] * column2[kd * 4 + ky]
                for kd in range(2)
                for ky in range(4)
                for at in (128 + (dx * 2 + kd) * 16 + kx * 4 + ky,)
            )
            for kx in range(4)
        ]
        for dx in range(2)
    ]
    for r in range(8):
        value = own2[r * 8:r * 8 + 8, :] + sum(
            in2[at:at + 1, :] * column2[kd * 4 + ky]
            for kd in range(2)
            for ky in range(4)
            for at in ((2 + kd) * 32 + ky * 8 + r,)
        )
        for dx, d in enumerate((1, -1)):
            if np.any(ux2[d][r] != 0.0):
                value = value + weighted(ux2[d][r], side2[dx])
        for b in range(2):
            for bz in range(2):
                at, part = 4 * (r // 4) + 2 * b + bz, value[4 * b:4 * b + 4, 64 * bz:64 * bz + 64]
                if at:
                    two[at - 1, r % 4] = part
                else:
                    approx[r % 4] = part


def store(approx_v, two_v, one_v, approx, two, one, sem):
    pairs = ((one_v, one), (two_v, two), (approx_v, approx))
    copies = [pltpu.make_async_copy(a, b, sem.at[k]) for k, (a, b) in enumerate(pairs)]
    for copy in copies:
        copy.start()
    for copy in copies:
        copy.wait()


def per_device(nx, ny, velocity):
    bx, by, nz = velocity.shape
    consts, levels_x, levels_y = tables(bx, by, nz)
    f32 = jnp.float32
    vmem = pl.BlockSpec(memory_space=pltpu.VMEM)
    held = [pltpu.VMEM(c.shape[-2:], f32) for c in consts]
    shapes = (
        (bx // 4, by // 4, nz // 4),
        (7, bx // 4, by // 4, nz // 4),
        (7, bx // 2, by // 2, nz // 2),
    )
    results = pl.pallas_call(
        functools.partial(kernel, nx, ny, levels_x, levels_y),
        out_shape=tuple(pltpu.VMEM(shape, f32) for shape in shapes),
        in_specs=[pl.BlockSpec(memory_space=pl.ANY)] * 5,
        out_specs=(vmem, vmem, vmem),
        scratch_shapes=[pltpu.VMEM((bx, by, nz), f32)]
        + held
        + [
            pltpu.VMEM((640, 128), f32),
            pltpu.VMEM((16, 2, 8, 256), f32),
            pltpu.VMEM((128, 256), f32),
            pltpu.VMEM((128, 256), f32),
            pltpu.VMEM((4, 4, 256), f32),
            pltpu.VMEM((4, 4, 256), f32),
            pltpu.VMEM((192, 128), f32),
            pltpu.VMEM((192, 128), f32),
            pltpu.SemaphoreType.DMA((7,)),
        ]
        + [pltpu.SemaphoreType.DMA((8,))] * 4,
        compiler_params=pltpu.CompilerParams(
            collective_id=0, has_side_effects=True, vmem_limit_bytes=60 * 1024 * 1024
        ),
    )(velocity, *[jnp.asarray(c) for c in consts])
    results = [pltpu.with_memory_space_constraint(r, pltpu.VMEM) for r in results]
    return pl.pallas_call(
        store,
        out_shape=tuple(jax.ShapeDtypeStruct(shape, f32) for shape in shapes),
        in_specs=[vmem] * 3,
        out_specs=[pl.BlockSpec(memory_space=pl.ANY)] * 3,
        scratch_shapes=[pltpu.SemaphoreType.DMA((3,))],
    )(*results)


def solution(mesh):
    placed = (P("slab", "morton", None),)
    return jax.shard_map(
        functools.partial(per_device, mesh.shape["slab"], mesh.shape["morton"]),
        mesh=mesh,
        in_specs=placed,
        out_specs=(
            P("slab", "morton", None),
            P(None, "slab", "morton", None),
            P(None, "slab", "morton", None),
        ),
        check_vma=False,
    )
```

```python
import functools

import jax
import jax.numpy as jnp
import numpy as np
from jax import lax
from jax.experimental import pallas as pl
from jax.experimental.pallas import tpu as pltpu
from jax.sharding import PartitionSpec as P

LIFT_ALPHA = -1.586134342059924
LIFT_BETA = -0.052980118572961
LIFT_GAMMA = 0.882911075530934
LIFT_DELTA = 0.443506852043971
LIFT_SCALE = 1.149604398860241

MESH = pl.DeviceIdType.MESH
FACES = ((1, 0), (-1, 0), (0, 1), (0, -1))
CORNERS = ((1, 1), (1, -1), (-1, 1), (-1, -1))
WAYS = FACES + CORNERS
ORDER = (7, 3, 5, 1, 6, 0, 2, 4)
HIGHEST = lax.Precision.HIGHEST


def lift_matrix(n):
    x = np.pad(np.eye(n), ((4, 4), (0, 0)), mode="reflect")
    e, o = x[0::2], x[1::2]
    d1 = o[:-1] + LIFT_ALPHA * (e[:-1] + e[1:])
    s1 = e[1:-1] + LIFT_BETA * (d1[:-1] + d1[1:])
    d2 = d1[1:-1] + LIFT_GAMMA * (s1[:-1] + s1[1:])
    s2 = s1[1:-1] + LIFT_DELTA * (d2[:-1] + d2[1:])
    return s2 * LIFT_SCALE, d2[1:] / LIFT_SCALE


def low_rank(coupling, rank):
    rest, us, vs = coupling.copy(), [], []
    for _ in range(rank):
        i, j = np.unravel_index(np.argmax(np.abs(rest)), rest.shape)
        u, v = rest[:, j] / rest[i, j], rest[i, :].copy()
        us.append(u)
        vs.append(v)
        rest = rest - u[:, None] * v[None, :]
    assert np.abs(rest).max() < 1e-12
    return np.stack(us, 1), np.stack(vs, 0)


def block_maps(b):
    blocks = 5
    low, high = lift_matrix(blocks * b)
    low2, high2 = lift_matrix(blocks * b // 2)
    pairs = ((low, high, 2), (low2 @ low, high2 @ low, 4))
    levels = []
    for lows, highs, rank in pairs:
        n = lows.shape[0] // blocks

        def part(row, col):
            cols = slice(col * b, (col + 1) * b)
            rows = slice(row * n, (row + 1) * n)
            return np.concatenate([lows[rows, cols], highs[rows, cols]])

        for row in range(blocks):
            for col in range(blocks):
                if abs(row - col) > 1:
                    assert np.abs(part(row, col)).max() == 0
                elif row != col:
                    like = part(2, 2 + col - row)
                    assert np.abs(part(row, col) - like).max() < 1e-12
        assert np.abs(part(1, 1) - part(2, 2)).max() < 1e-12
        assert np.abs(part(3, 3) - part(2, 2)).max() < 1e-12
        own = [part(0, 0), part(2, 2), part(4, 4)]
        u_up, v_up = low_rank(part(2, 1), rank)
        u_down, v_down = low_rank(part(2, 3), rank)
        levels.append((own, {1: u_up, -1: u_down}, {1: v_up, -1: v_down}))
    return levels


@functools.lru_cache(maxsize=None)
def tables(bx, by, nz):
    low, high = lift_matrix(nz)
    low2, high2 = lift_matrix(nz // 2)
    depth1 = np.concatenate([low, high]).T
    depth2 = np.concatenate([low2, high2]).T
    levels_x, levels_y = block_maps(bx), block_maps(by)
    own_x, ux, vx = levels_x[1]
    own_y, uy, vy = levels_y[1]
    nx, ny = own_x[0].shape[0], own_y[0].shape[0]
    plane = []
    for cx in range(3):
        for cy in range(3):
            out = []
            for dx, dy in WAYS:
                m = np.kron(vx[dx] if dx else own_x[cx], vy[dy] if dy else own_y[cy])
                if dx == 0:
                    m = m.reshape(nx, -1, bx * by).transpose(1, 0, 2).reshape(-1, bx * by)
                out.append(m)
            out.append(np.kron(own_x[cx], own_y[cy]))
            plane.append(np.concatenate(out))
    columns = np.concatenate([u[d].T.reshape(-1) for u in (levels_y[0][1], uy) for d in (1, -1)])
    columns = np.repeat(columns[:, None], 128, axis=1)
    arrays = [t.astype(np.float32) for t in (depth1, depth2, np.stack(plane), columns)]
    return arrays, levels_x, levels_y


def dot(a, b):
    return jnp.dot(a, b, precision=HIGHEST, preferred_element_type=jnp.float32)


def lift_ends(e, o, prev, after, first, last):
    at, sub = jnp.where, lambda f, *lists: [f(*v) for v in zip(*lists)]
    e_after = after(e, sub(lambda p: at(last, p, 0.0), e))
    d1 = sub(lambda p, q, r: p + LIFT_ALPHA * (q + r), o, e, e_after)
    out1 = sub(lambda p: LIFT_ALPHA * p, e)
    d1_prev = prev(d1, sub(lambda p, q: at(first, p, q), d1, out1))
    s1 = sub(lambda p, q, r: p + LIFT_BETA * (q + r), e, d1_prev, d1)
    s1_after = after(s1, sub(lambda p, q: at(last, p, LIFT_BETA * q), s1, d1))
    d2 = sub(lambda p, q, r: p + LIFT_GAMMA * (q + r), d1, s1, s1_after)
    out2 = sub(lambda p, q: p + LIFT_GAMMA * (LIFT_BETA * p + q), out1, s1)
    d2_prev = prev(d2, sub(lambda p, q: at(first, p, q), d2, out2))
    s2 = sub(lambda p, q, r: p + LIFT_DELTA * (q + r), s1, d2_prev, d2)
    return [v * LIFT_SCALE for v in s2], [v * (1.0 / LIFT_SCALE) for v in d2]


def weighted(weights, values):
    terms = [float(w) * v for w, v in zip(weights, values) if w != 0.0]
    return functools.reduce(lambda p, q: p + q, terms)


def kernel(
    nx, ny, levels_x, levels_y, x_hbm, t1_hbm, t2_hbm, s2_hbm, uy_hbm, approx, two, one,
    x_v, t1_v, t2_v, s2_v, uy_v, xb, own1,
    face1_out, face1_in, corner1_out, corner1_in, out2, in2,
    load_sem, send1, recv1, send2, recv2,
):
    px, py = lax.axis_index("slab"), lax.axis_index("morton")
    not_first_x, last_x = lax.div(px + (nx - 2), nx - 1), lax.div(px, nx - 1)
    not_first_y, last_y = lax.div(py + (ny - 2), ny - 1), lax.div(py, ny - 1)
    here = (not_first_x + last_x) * 3 + not_first_y + last_y
    has_x = {1: 1 - last_x, -1: not_first_x, 0: 1}
    has_y = {1: 1 - last_y, -1: not_first_y, 0: 1}

    def exists(dx, dy):
        return has_x[dx] * has_y[dy] == 1

    def rows(ref, start, size):
        return ref.at[pl.ds(start, size)]

    loads = [
        pltpu.make_async_copy(source, target, load_sem.at[k])
        for k, (source, target) in enumerate((
            (x_hbm, x_v),
            (t1_hbm, t1_v),
            (t2_hbm, t2_v),
            (s2_hbm.at[here], s2_v),
            (uy_hbm, uy_v),
        ))
    ]
    for load in loads:
        load.start()

    barrier = pltpu.get_barrier_semaphore()
    for dx, dy in WAYS:
        @pl.when(exists(dx, dy))
        def _():
            pl.semaphore_signal(
                barrier, inc=1, device_id=(py + dy, px + dx), device_id_type=MESH
            )

    def message(level, k):
        dx, dy = WAYS[k]
        if level == 1 and k < 4:
            pair = rows(face1_out, k * 32, 32), rows(face1_in, k * 32, 32)
        elif level == 1:
            pair = corner1_out.at[k - 4], corner1_in.at[k - 4]
        elif k < 4:
            pair = rows(out2, k * 32, 32), rows(in2, k * 32, 32)
        else:
            pair = rows(out2, 64 + k * 16, 16), rows(in2, 64 + k * 16, 16)
        send, recv = (send1, recv1) if level == 1 else (send2, recv2)
        return pltpu.make_async_remote_copy(
            src_ref=pair[0],
            dst_ref=pair[1],
            send_sem=send.at[k],
            recv_sem=recv.at[k],
            device_id=(py + dy, px + dx),
            device_id_type=MESH,
        )

    def start(level):
        for k in ORDER:
            @pl.when(exists(*WAYS[k]))
            def _():
                message(level, k).start()

    def receive(level):
        for k in ORDER:
            dx, dy = WAYS[k]

            @pl.when(exists(-dx, -dy))
            def _():
                message(level, k).wait_recv()

    for k, (dx, dy) in enumerate(WAYS):
        @pl.when(jnp.logical_not(exists(-dx, -dy)))
        def _():
            if k < 4:
                face1_in[k * 32:k * 32 + 32, :] = jnp.zeros((32, 256), jnp.float32)
                in2[k * 32:k * 32 + 32, :] = jnp.zeros((32, 128), jnp.float32)
            else:
                corner1_in[k - 4] = jnp.zeros((4, 256), jnp.float32)
                in2[64 + k * 16:80 + k * 16, :] = jnp.zeros((16, 128), jnp.float32)

    loads[0].wait()
    loads[1].wait()
    z1 = dot(x_v[...].reshape(256, 256), t1_v[...])

    planes = [z1[16 * i:16 * i + 16, :] for i in range(16)]
    low, high = lift_ends(
        planes[0::2], planes[1::2],
        lambda v, end: [end[0]] + v[:-1],
        lambda v, end: v[1:] + [end[-1]],
        not_first_x == 0, last_x == 1,
    )
    _, ux, vx = levels_x[0]
    _, uy, vy = levels_y[0]
    along = [weighted(w, planes) for d in (1, -1) for w in vx[d]]
    for r, v in enumerate(low + high + along):
        for h in range(2):
            xb[320 * h + 16 * r:320 * h + 16 * r + 16, :] = v[:, 128 * h:128 * h + 128]

    def strided(begin, size, stride):
        return jnp.concatenate(
            [xb[pl.ds(320 * h + begin, size, stride=stride), :] for h in range(2)], axis=1
        )

    for kd, d in enumerate((1, -1)):
        for ky in range(2):
            taps = [y for y in range(16) if vy[d][ky, y] != 0.0]
            weights = [vy[d][ky, y] for y in taps]
            at = (2 + kd) * 32 + ky * 16
            face1_out[at:at + 16, :] = weighted(
                weights, [strided(y, 16, 16) for y in taps]
            )
            part = weighted(weights, [strided(256 + y, 4, 16) for y in taps])
            corner1_out[kd, 2 * ky:2 * ky + 2, :] = part[0:2]
            corner1_out[2 + kd, 2 * ky:2 * ky + 2, :] = part[2:4]

    place = lax.broadcasted_iota(jnp.int32, (8, 256), 0)
    for r in (16, 17, 18, 19) + tuple(range(16)):
        low, high = lift_ends(
            [strided(16 * r, 8, 2)], [strided(16 * r + 1, 8, 2)],
            lambda v, end: [jnp.where(place == 0, end[0], pltpu.roll(v[0], 1, 0))],
            lambda v, end: [jnp.where(place == 7, end[0], pltpu.roll(v[0], 7, 0))],
            not_first_y == 0, last_y == 1,
        )
        if r >= 16:
            at = (r - 16) * 16
            face1_out[at:at + 8, :] = low[0]
            face1_out[at + 8:at + 16, :] = high[0]
        else:
            own1[r, 0] = low[0]
            own1[r, 1] = high[0]
        if r == 19:
            pl.semaphore_wait(
                barrier,
                (1 + has_x[1] + has_x[-1]) * (1 + has_y[1] + has_y[-1]) - 1,
            )
            start(1)

    loads[2].wait()
    z2 = dot(z1[:, :128], t2_v[...])
    loads[3].wait()
    out2[...] = dot(s2_v[:192, :], z2)
    start(2)
    own2 = dot(s2_v[192:, :], z2)
    loads[4].wait()

    receive(1)
    for bz in range(2):
        half = slice(bz * 128, bz * 128 + 128)
        column = [[[
            uy_v[((kd * 2 + ky) * 2 + b) * 8:((kd * 2 + ky) * 2 + b) * 8 + 8, :]
            for b in range(2)] for ky in range(2)] for kd in range(2)]

        def add_y(value, row, b):
            for kd in range(2):
                for ky in range(2):
                    value = value + row(kd, ky) * column[kd][ky][b]
            return value

        for b in range(2):
            side = [
                [
                    add_y(
                        face1_in[dx * 32 + kx * 16 + b * 8:dx * 32 + kx * 16 + b * 8 + 8, half],
                        lambda kd, ky: corner1_in[dx * 2 + kd, 2 * ky + kx:2 * ky + kx + 1, half],
                        b,
                    )
                    for kx in range(2)
                ]
                for dx in range(2)
            ]
            for r in range(16):
                band, i = 2 * (r // 8) + b, r % 8
                if band + bz == 0:
                    continue
                value = add_y(
                    own1[r, b, :, half],
                    lambda kd, ky: face1_in[
                        (2 + kd) * 32 + ky * 16 + r:(2 + kd) * 32 + ky * 16 + r + 1, half
                    ],
                    b,
                )
                for dx, d in enumerate((1, -1)):
                    if np.any(ux[d][r] != 0.0):
                        value = value + weighted(ux[d][r], side[dx])
                one[2 * band + bz - 1, i] = value

    receive(2)
    _, ux2, _ = levels_x[1]
    column2 = [uy_v[64 + k * 8:72 + k * 8, :] for k in range(8)]
    side2 = [
        [
            in2[dx * 32 + kx * 8:dx * 32 + kx * 8 + 8, :]
            + sum(
                in2[at:at + 1, :] * column2[kd * 4 + ky]
                for kd in range(2)
                for ky in range(4)
                for at in (128 + (dx * 2 + kd) * 16 + kx * 4 + ky,)
            )
            for kx in range(4)
        ]
        for dx in range(2)
    ]
    for r in range(8):
        value = own2[r * 8:r * 8 + 8, :] + sum(
            in2[at:at + 1, :] * column2[kd * 4 + ky]
            for kd in range(2)
            for ky in range(4)
            for at in ((2 + kd) * 32 + ky * 8 + r,)
        )
        for dx, d in enumerate((1, -1)):
            if np.any(ux2[d][r] != 0.0):
                value = value + weighted(ux2[d][r], side2[dx])
        for b in range(2):
            for bz in range(2):
                at, part = 4 * (r // 4) + 2 * b + bz, value[4 * b:4 * b + 4, 64 * bz:64 * bz + 64]
                if at:
                    two[at - 1, r % 4] = part
                else:
                    approx[r % 4] = part

    for level in (1, 2):
        for k in ORDER:
            @pl.when(exists(*WAYS[k]))
            def _():
                message(level, k).wait_send()


def store(approx_v, two_v, one_v, approx, two, one, sem):
    pairs = ((one_v, one), (two_v, two), (approx_v, approx))
    copies = [pltpu.make_async_copy(a, b, sem.at[k]) for k, (a, b) in enumerate(pairs)]
    for copy in copies:
        copy.start()
    for copy in copies:
        copy.wait()


def per_device(nx, ny, velocity):
    bx, by, nz = velocity.shape
    consts, levels_x, levels_y = tables(bx, by, nz)
    f32 = jnp.float32
    vmem = pl.BlockSpec(memory_space=pltpu.VMEM)
    held = [pltpu.VMEM(c.shape[-2:], f32) for c in consts]
    shapes = (
        (bx // 4, by // 4, nz // 4),
        (7, bx // 4, by // 4, nz // 4),
        (7, bx // 2, by // 2, nz // 2),
    )
    results = pl.pallas_call(
        functools.partial(kernel, nx, ny, levels_x, levels_y),
        out_shape=tuple(pltpu.VMEM(shape, f32) for shape in shapes),
        in_specs=[pl.BlockSpec(memory_space=pl.ANY)] * 5,
        out_specs=(vmem, vmem, vmem),
        scratch_shapes=[pltpu.VMEM((bx, by, nz), f32)]
        + held
        + [
            pltpu.VMEM((640, 128), f32),
            pltpu.VMEM((16, 2, 8, 256), f32),
            pltpu.VMEM((128, 256), f32),
            pltpu.VMEM((128, 256), f32),
            pltpu.VMEM((4, 4, 256), f32),
            pltpu.VMEM((4, 4, 256), f32),
            pltpu.VMEM((192, 128), f32),
            pltpu.VMEM((192, 128), f32),
            pltpu.SemaphoreType.DMA((5,)),
        ]
        + [pltpu.SemaphoreType.DMA((8,))] * 4,
        compiler_params=pltpu.CompilerParams(
            collective_id=0, has_side_effects=True, vmem_limit_bytes=60 * 1024 * 1024
        ),
    )(velocity, *[jnp.asarray(c) for c in consts])
    results = [pltpu.with_memory_space_constraint(r, pltpu.VMEM) for r in results]
    return pl.pallas_call(
        store,
        out_shape=tuple(jax.ShapeDtypeStruct(shape, f32) for shape in shapes),
        in_specs=[vmem] * 3,
        out_specs=[pl.BlockSpec(memory_space=pl.ANY)] * 3,
        scratch_shapes=[pltpu.SemaphoreType.DMA((3,))],
    )(*results)


def solution(mesh):
    placed = (P("slab", "morton", None),)
    return jax.shard_map(
        functools.partial(per_device, mesh.shape["slab"], mesh.shape["morton"]),
        mesh=mesh,
        in_specs=placed,
        out_specs=(
            P("slab", "morton", None),
            P(None, "slab", "morton", None),
            P(None, "slab", "morton", None),
        ),
        check_vma=False,
    )
```
